32 devices in a mesh: ctx: 2 (over x), head: 4 (over y, core), rep: 4 (over z).
Axes of the slice: x: 2, y: 2, z: 4, core: 2. Of those that a mesh axis runs over, the one named last changes fastest.
Arguments:
- tokens: bfloat16 [4, 256, 4096], P('rep', 'ctx'), may hold values from -6 to 6
- queries: bfloat16 [4, 256, 4096], P('rep', 'ctx', 'head'), may hold values from -40 to 40
- cotangent: bfloat16 [4, 256, 4096], P('rep', 'ctx', 'head'), may hold values from -0.19921875 to 0.19921875
- key_weight: bfloat16 [4096, 1024], P('ctx', 'head'), may hold values from -0.09375 to 0.09375
- value_weight: bfloat16 [4096, 1024], P('ctx', 'head'), may hold values from -0.09375 to 0.09375
- probe: int32 [2, 4096, 1024], P(None, None, 'head'), may hold values from -1 to 1, as said below
Outputs:
- curvature: float32 [2, 4096, 1024], P(None, 'ctx', 'head')
The draws below stay inside these ranges and needn't reach their ends.
Inputs may be any that keep to these rules, and one draw needn't show every extreme that they name: `probe`: every entry is -1 or 1.
All inputs are finite; a program needn't handle non-finite values.
Results may differ from the reference program's by a relative error of at most 0.0095.
The reference program's roundings to bfloat16 on the way (of `grads`) count: a program that leaves them out, or rounds other values in their place, can miss the bound.
Values may be sent and summed in bfloat16 or wider, within the bound.
A program may use at most 128 MiB of HBM per device.

```python
import jax
import jax.numpy as jnp
from jax import lax

D = 4096
HEADS = 32
KV_HEADS = 8
HEAD_DIM = 128
SEQ = 256
REPS = 4


def draw_queries(key, part):
    key = jax.random.fold_in(key, 11)
    shape = (REPS, SEQ, HEADS * HEAD_DIM)
    base = jnp.clip(jax.random.normal(key, shape, jnp.float32), -4.0, 4.0)
    return base.astype(jnp.bfloat16)


def draw_probe(key, part):
    key = jax.random.fold_in(key, 23)
    coins = jax.random.randint(key, (2, D, KV_HEADS * HEAD_DIM), 0, 2)
    return (2 * coins - 1).astype(jnp.int32)


def with_spikes(result, stream_key, source, target, parts, factor):
    def block_of(axis_at):
        return (jnp.arange(result.shape[axis_at]) // (result.shape[axis_at] // parts)).reshape((-1,) + (1,) * (result.ndim - 1 - axis_at))

    near = jax.random.permutation(stream_key, parts)[block_of(target)]
    far = (block_of(target) + parts // 2) % parts
    return jnp.where((block_of(source) == near) | (block_of(source) == far), factor * result, result)


def block_scale(stream_key, dims, pieces, smallest, largest):
    loudness = 1.0
    for axis_at, shards_of in pieces:
        heights = jax.random.uniform(jax.random.fold_in(jax.random.fold_in(stream_key, 6), axis_at), (shards_of,), jnp.float32, smallest / len(pieces), largest / len(pieces))
        loudness = loudness * jnp.repeat(jnp.exp(heights), dims[axis_at] // shards_of).reshape((-1,) + (1,) * (len(dims) - 1 - axis_at))
    return loudness


def gaussian(rng, shape, deviation, most, shards=(), kind=jnp.bfloat16):
    gain = block_scale(rng, shape, shards, -0.22, 0.18) if shards else 1.0
    values = jax.random.normal(rng, shape, jnp.float32) * deviation * gain
    return jnp.minimum(jnp.maximum(values, -most), most).astype(kind)


def bell_draw_with(own_key, shape, scale, bound, cuts, heavy, kind=jnp.bfloat16):
    result = scale * jax.random.normal(own_key, shape, jnp.float32)
    if cuts:
        result = result * block_scale(own_key, shape, cuts, -0.22, 0.18)
    return jnp.clip(with_spikes(result, jax.random.fold_in(own_key, 3), *heavy), -bound, bound).astype(kind)


def setup_inputs(seed: int = 0) -> dict:
    key_of = jax.random.split(jax.random.key(seed), 7)
    tokens = bell_draw_with(key_of[0], (REPS, SEQ, D), 1.0, 6.0, ((0, 4), (1, 2)), (1, 2, 2, 2.0))
    queries = draw_queries(jax.random.fold_in(key_of[6], 71), 0)
    cotangent = gaussian(key_of[2], (REPS, SEQ, HEADS * HEAD_DIM), 0.03, 0.19921875, ((0, 4), (1, 2), (2, 4)))
    key_weight = gaussian(key_of[3], (D, KV_HEADS * HEAD_DIM), D ** -0.5, 0.09375, ((0, 2), (1, 4)))
    value_weight = gaussian(key_of[4], (D, KV_HEADS * HEAD_DIM), D ** -0.5, 0.09375, ((0, 2), (1, 4)))
    probe = draw_probe(jax.random.fold_in(key_of[6], 71), 0)
    return {"tokens": tokens, "queries": queries, "cotangent": cotangent, "key_weight": key_weight, "value_weight": value_weight, "probe": probe}


NEG_FILL = -1.0e30


def times_t(left, right):
    return lax.dot_general(left, right, (((1,), (1,)), ((), ())), preferred_element_type=jnp.float32)


def times_tn(left, right):
    return lax.dot_general(left, right, (((0,), (0,)), ((), ())), preferred_element_type=jnp.float32)


def head_terms(query_rows, cot_rows, keys, values, tan_keys, tan_values):
    scaling = HEAD_DIM ** -0.5
    group = HEADS // KV_HEADS
    query_pos = jnp.arange(query_rows.shape[0], dtype=jnp.int32) // group
    key_pos = jnp.arange(keys.shape[0], dtype=jnp.int32)
    valid = key_pos[None, :] <= query_pos[:, None]
    scores = jnp.where(valid, scaling * times_t(query_rows, keys), NEG_FILL)
    tan_scores = scaling * times_t(query_rows, tan_keys)
    peak = jnp.max(scores, axis=1)
    expo = jnp.exp(scores - peak[:, None])
    total = jnp.sum(expo, axis=1)
    along = jnp.sum(expo * tan_scores, axis=1)
    expo_half = expo.astype(jnp.bfloat16)
    acc_value = jnp.dot(expo_half, values, preferred_element_type=jnp.float32)
    acc_mixed = jnp.dot((expo * tan_scores).astype(jnp.bfloat16), values, preferred_element_type=jnp.float32)
    acc_tan = jnp.dot(expo_half, tan_values, preferred_element_type=jnp.float32)
    output = acc_value / total[:, None]
    shift_mean = along / total
    tan_output = (acc_mixed - shift_mean[:, None] * acc_value) / total[:, None] + acc_tan / total[:, None]
    cot_float = cot_rows.astype(jnp.float32)
    delta = jnp.sum(cot_float * output, axis=1)
    tan_delta = jnp.sum(cot_float * tan_output, axis=1)
    probs = expo / total[:, None]
    tan_probs = probs * (tan_scores - shift_mean[:, None])
    value_terms = times_tn(tan_probs.astype(jnp.bfloat16), cot_rows)
    dprob = times_t(cot_rows, values)
    tan_dprob = times_t(cot_rows, tan_values)
    tan_dscore = tan_probs * (dprob - delta[:, None]) + probs * (tan_dprob - tan_delta[:, None])
    key_terms = scaling * times_tn(tan_dscore.astype(jnp.bfloat16), query_rows)
    return key_terms, value_terms


def reference(tokens, queries, cotangent, key_weight, value_weight, probe):
    sign = probe.astype(jnp.float32).astype(jnp.bfloat16)
    group = HEADS // KV_HEADS

    def split_heads(block):
        return block.reshape(SEQ, KV_HEADS, HEAD_DIM).transpose(1, 0, 2)

    def split_queries(block):
        return block.reshape(SEQ, KV_HEADS, group * HEAD_DIM).transpose(1, 0, 2).reshape(KV_HEADS, SEQ * group, HEAD_DIM)

    def replica(items):
        tok, query_block, cot_block = items
        keys = jnp.dot(tok, key_weight, preferred_element_type=jnp.float32).astype(jnp.bfloat16)
        values = jnp.dot(tok, value_weight, preferred_element_type=jnp.float32).astype(jnp.bfloat16)
        tan_keys = jnp.dot(tok, sign[0], preferred_element_type=jnp.float32).astype(jnp.bfloat16)
        tan_values = jnp.dot(tok, sign[1], preferred_element_type=jnp.float32).astype(jnp.bfloat16)
        head_items = (split_queries(query_block), split_queries(cot_block), split_heads(keys),
                      split_heads(values), split_heads(tan_keys), split_heads(tan_values))
        key_terms, value_terms = lax.map(lambda item: head_terms(*item), head_items)
        key_flat = key_terms.transpose(1, 0, 2).reshape(SEQ, KV_HEADS * HEAD_DIM)
        value_flat = value_terms.transpose(1, 0, 2).reshape(SEQ, KV_HEADS * HEAD_DIM)
        grads = jnp.concatenate([key_flat, value_flat], axis=1).astype(jnp.bfloat16)
        return times_tn(tok, grads)

    hvp = jnp.sum(lax.map(replica, (tokens, queries, cotangent)), axis=0)
    hvp = hvp.reshape(D, 2, KV_HEADS * HEAD_DIM).transpose(1, 0, 2)
    return probe.astype(jnp.float32) * hvp
```

```python
import functools

import jax
import jax.numpy as jnp
from jax import lax
from jax.experimental import pallas as pl
from jax.experimental.pallas import tpu as pltpu
from jax.sharding import PartitionSpec as P

HEADS = 32
KV_HEADS = 8
HEAD_DIM = 128


NEG_FILL = -1e30

BF16 = jnp.bfloat16
F32 = jnp.float32
CHUNKS = 4
N_REMOTE = 30


def times_t(left, right):
    return lax.dot_general(
        left, right, (((1,), (1,)), ((), ())), preferred_element_type=jnp.float32
    )


def times_tn(left, right):
    return lax.dot_general(
        left, right, (((0,), (0,)), ((), ())), preferred_element_type=jnp.float32
    )


def fused_kernel(tok, q, cot, kw, vw, probe, out,
                 gath, toks, qs, cots, kws, vws, signs, tan_own, tan_all,
                 part_own, part_in, grads, acc,
                 send_sem, recv_sem, local_sem, probe_sem, out_sem):
    x = lax.axis_index("ctx")
    h = lax.axis_index("head")
    z = lax.axis_index("rep")
    half = gath.shape[-1]
    rows = qs.shape[1]
    other = 1 - x
    sib = h + 1 - 2 * lax.rem(h, 2)
    yn = lax.rem(h + 2, 4)
    sib_yn = lax.rem(sib + 2, 4)
    zs = (z + 1 - 2 * lax.rem(z, 2), lax.rem(z + 2, 4), 3 - z)
    to_x = (other, h, z)
    to_s = (x, sib, z)
    to_y = (x, yn, z)
    to_z = tuple((x, h, zd) for zd in zs)

    def cols(index, width):
        return pl.ds(pl.multiple_of(index * width, width), width)

    loads = [
        pltpu.make_async_copy(tok, toks, local_sem.at[0]),
        pltpu.make_async_copy(tok.at[:, :, cols(x, half)], gath.at[z, :, x], local_sem.at[1]),
        pltpu.make_async_copy(kw, kws, local_sem.at[2]),
        pltpu.make_async_copy(vw, vws, local_sem.at[3]),
        pltpu.make_async_copy(q.at[:, cols(x, 512)], qs.at[x], local_sem.at[4]),
        pltpu.make_async_copy(cot.at[:, cols(x, 512)], cots.at[x], local_sem.at[5]),
    ]
    step = 2 * half // CHUNKS
    probes = [
        [
            pltpu.make_async_copy(
                probe.at[t, pl.ds(c * step, step)],
                signs.at[t, pl.ds(c * step, step)],
                probe_sem.at[t * CHUNKS + c],
            )
            for c in range(CHUNKS)
        ]
        for t in range(2)
    ]
    loads[0].start()
    for t in range(2):
        for c in range(CHUNKS):
            probes[t][c].start()
    for load in loads[1:]:
        load.start()

    barrier = pltpu.get_barrier_semaphore()
    for device in (to_x, to_s, to_y) + to_z:
        pl.semaphore_signal(barrier, inc=1, device_id=device, device_id_type=pl.DeviceIdType.MESH)
    pl.semaphore_wait(barrier, 6)

    sent = []

    def send(index, src, dst, device):
        copy = pltpu.make_async_remote_copy(
            src_ref=src, dst_ref=dst, send_sem=send_sem.at[index], recv_sem=recv_sem.at[index],
            device_id=device, device_id_type=pl.DeviceIdType.MESH,
        )
        copy.start()
        sent.append(copy)

    def arrive(index, slot, device):
        pltpu.make_async_remote_copy(
            src_ref=slot, dst_ref=slot, send_sem=send_sem.at[index], recv_sem=recv_sem.at[index],
            device_id=device, device_id_type=pl.DeviceIdType.MESH,
        ).wait_recv()

    send(0, tok.at[h, :, cols(other, half)], gath.at[z, h, x], to_x)
    for d in range(3):
        send(1 + d, tok.at[h, :, cols(x, half)], gath.at[z, h, x], to_z[d])
    send(19, q.at[:, cols(other, 512)], qs.at[x], to_x)
    send(20, cot.at[:, cols(other, 512)], cots.at[x], to_x)

    def project_tangent(t):
        total = jnp.zeros((rows, 256), F32)
        for c in range(CHUNKS):
            probes[t][c].wait()
            sign = signs[t, pl.ds(c * step, step), :].astype(F32).astype(BF16)
            block = toks[:, :, pl.ds(c * step, step)].reshape(rows, step)
            total = total + jnp.dot(block, sign, preferred_element_type=F32)
        half_total = total.astype(BF16)
        for j in range(2):
            tan_own[j, :, :, t * 128:(t + 1) * 128] = half_total[:, j * 128:(j + 1) * 128].reshape(4, rows // 4, 128)

    loads[0].wait()
    project_tangent(0)
    arrive(0, gath.at[z, h, other], to_x)
    send(7, gath.at[z, h, other], gath.at[z, h, other], to_y)
    send(8, gath.at[z, h, other], gath.at[z, h, other], to_s)
    for d in range(3):
        send(4 + d, gath.at[z, h, other], gath.at[z, h, other], to_z[d])
    project_tangent(1)
    send(21, tan_own.at[other], tan_all.at[:, x], to_x)
    arrive(7, gath.at[z, yn, other], to_y)
    send(9, gath.at[z, yn, other], gath.at[z, yn, other], to_s)
    tan_all[:, pl.ds(x, 1)] = tan_own[x][:, None]
    arrive(8, gath.at[z, sib, other], to_s)
    arrive(9, gath.at[z, sib_yn, other], to_s)
    for index in (1, 2, 3):
        loads[index].wait()
    seq = 2 * rows
    mine = gath[z].reshape(seq, half)
    for t, weight in enumerate((kws, vws)):
        partial = jnp.dot(mine, weight[...], preferred_element_type=F32)
        for j in range(2):
            part_own[j, :, t * 128:(t + 1) * 128] = partial[:, j * 128:(j + 1) * 128]
    send(22, part_own.at[other], part_in, to_x)

    def pass_rep(d):
        arrive(1 + d, gath.at[zs[d], h, x], to_z[d])
        arrive(4 + d, gath.at[zs[d], h, other], to_z[d])
        send(10 + d, gath.at[zs[d], h], gath.at[zs[d], h], to_y)
        send(13 + d, gath.at[zs[d], h], gath.at[zs[d], h], to_s)

    def pass_sibling(d):
        arrive(10 + d, gath.at[zs[d], yn], to_y)
        send(16 + d, gath.at[zs[d], yn], gath.at[zs[d], yn], to_s)

    pass_rep(0)
    pass_rep(1)
    loads[4].wait()
    loads[5].wait()
    arrive(19, qs.at[other], to_x)
    arrive(20, cots.at[other], to_x)
    arrive(21, tan_all.at[:, other], to_x)
    arrive(22, part_in, to_x)

    both = (part_own[x] + part_in[...]).astype(BF16)
    keys, values = both[:, :128], both[:, 128:]
    tangents = tan_all[...].reshape(seq, 256)
    tan_keys, tan_values = tangents[:, :128], tangents[:, 128:]
    scaling = HEAD_DIM ** (-0.5)
    quarter = rows // 4
    slot = lax.broadcasted_iota(jnp.int32, (seq, seq), 1)
    key_pos = (
        lax.rem(lax.div(slot, quarter), 2) * rows
        + lax.div(slot, 2 * quarter) * quarter
        + lax.rem(slot, quarter)
    )
    valid = key_pos <= lax.broadcasted_iota(jnp.int32, (seq, seq), 0)
    key_terms = jnp.zeros((seq, 128), F32)
    value_terms = jnp.zeros((seq, 128), F32)
    hooks = (lambda: pass_rep(2), lambda: pass_sibling(0), lambda: pass_sibling(1), lambda: None)
    for g in range(4):
        hooks[g]()
        span = slice(g * 128, (g + 1) * 128)
        query = qs[:, :, span].reshape(seq, 128)
        cotan = cots[:, :, span].reshape(seq, 128)
        scores = jnp.where(valid, scaling * times_t(query, keys), NEG_FILL)
        tan_scores = scaling * times_t(query, tan_keys)
        peak = jnp.max(scores, axis=1, keepdims=True)
        expo = jnp.exp(scores - peak)
        total = jnp.sum(expo, axis=1, keepdims=True)
        mixed = expo * tan_scores
        along = jnp.sum(mixed, axis=1, keepdims=True)
        expo_half = expo.astype(BF16)
        acc_value = jnp.dot(expo_half, values, preferred_element_type=F32)
        acc_mixed = jnp.dot(mixed.astype(BF16), values, preferred_element_type=F32)
        acc_tan = jnp.dot(expo_half, tan_values, preferred_element_type=F32)
        inverse = 1.0 / total
        shift_mean = along * inverse
        tan_sum = acc_mixed - shift_mean * acc_value + acc_tan
        cot_float = cotan.astype(F32)
        delta = jnp.sum(cot_float * acc_value, axis=1, keepdims=True) * inverse
        tan_delta = jnp.sum(cot_float * tan_sum, axis=1, keepdims=True) * inverse
        probs = expo * inverse
        tan_probs = probs * (tan_scores - shift_mean)
        dprob = times_t(cotan, values)
        tan_dprob = times_t(cotan, tan_values)
        tan_dscore = tan_probs * (dprob - delta) + probs * (tan_dprob - tan_delta)
        value_terms = value_terms + times_tn(tan_probs.astype(BF16), cotan)
        key_terms = key_terms + times_tn(tan_dscore.astype(BF16), query)
    own = cols(x, 128)
    theirs = cols(other, 128)
    grads[z, 0, :, own] = (scaling * key_terms).astype(BF16)
    grads[z, 1, :, own] = value_terms.astype(BF16)
    mine_at = grads.at[z, :, :, own]
    for d in range(3):
        send(24 + d, mine_at, mine_at, to_z[d])
    send(23, mine_at, mine_at, to_x)
    pass_sibling(2)
    for d in range(3):
        arrive(13 + d, gath.at[zs[d], sib], to_s)
        arrive(16 + d, gath.at[zs[d], sib_yn], to_s)

    block = 256
    blocks = half // block

    def product(rep, start, t):
        left = gath[rep, :, :, :, pl.ds(start, block)].reshape(seq, block)
        return times_tn(left, grads[rep, t])

    def pass_grads(d):
        at = grads.at[zs[d], :, :, own]
        arrive(24 + d, at, to_z[d])
        send(27 + d, at, at, to_x)

    def add_rep(rep, first):
        @pl.loop(0, blocks)
        def _(i):
            start = pl.multiple_of(i * block, block)
            for t in range(2):
                value = product(rep, start, t)
                if not first:
                    value = value + acc[t, pl.ds(start, block), :]
                acc[t, pl.ds(start, block), :] = value

    pass_grads(0)
    arrive(23, grads.at[z, :, :, theirs], to_x)
    add_rep(z, True)
    pass_grads(1)
    pass_grads(2)
    arrive(27, grads.at[zs[0], :, :, theirs], to_x)
    add_rep(zs[0], False)
    arrive(28, grads.at[zs[1], :, :, theirs], to_x)
    add_rep(zs[1], False)
    arrive(29, grads.at[zs[2], :, :, theirs], to_x)

    def write(i):
        start = pl.multiple_of(i * block, block)
        return pltpu.make_async_copy(
            acc.at[:, pl.ds(start, block)], out.at[:, pl.ds(start, block)], out_sem.at[i]
        )

    @pl.loop(0, blocks)
    def _(i):
        start = pl.multiple_of(i * block, block)
        for t in range(2):
            value = product(zs[2], start, t) + acc[t, pl.ds(start, block), :]
            sign_at = pl.multiple_of(x * half + i * block, block)
            acc[t, pl.ds(start, block), :] = value * signs[t, pl.ds(sign_at, block), :].astype(F32)
        write(i).start()

    @pl.loop(0, blocks)
    def _(i):
        write(i).wait()

    for copy in sent:
        copy.wait_send()


def fused(tokens, queries, cotangent, key_weight, value_weight, probe):
    _, rows, depth = tokens.shape
    half = key_weight.shape[0]
    any_spec = pl.BlockSpec(memory_space=pl.ANY)
    return pl.pallas_call(
        fused_kernel,
        out_shape=jax.ShapeDtypeStruct((2, half, 256), F32),
        in_specs=[any_spec] * 6,
        out_specs=any_spec,
        scratch_shapes=[
            pltpu.VMEM((4, 4, 2, rows // 4, half), BF16),
            pltpu.VMEM((4, rows // 4, depth), BF16),
            pltpu.VMEM((2, rows, 512), BF16),
            pltpu.VMEM((2, rows, 512), BF16),
            pltpu.VMEM((half, 256), BF16),
            pltpu.VMEM((half, 256), BF16),
            pltpu.VMEM((2, depth, 256), jnp.int32),
            pltpu.VMEM((2, 4, rows // 4, 256), BF16),
            pltpu.VMEM((4, 2, rows // 4, 256), BF16),
            pltpu.VMEM((2, 2 * rows, 256), F32),
            pltpu.VMEM((2 * rows, 256), F32),
            pltpu.VMEM((4, 2, 2 * rows, 256), BF16),
            pltpu.VMEM((2, half, 256), F32),
            pltpu.SemaphoreType.DMA((N_REMOTE,)),
            pltpu.SemaphoreType.DMA((N_REMOTE,)),
            pltpu.SemaphoreType.DMA((6,)),
            pltpu.SemaphoreType.DMA((2 * CHUNKS,)),
            pltpu.SemaphoreType.DMA((half // 256,)),
        ],
        compiler_params=pltpu.CompilerParams(
            collective_id=0, has_side_effects=True, vmem_limit_bytes=56 * 1024 * 1024
        ),
        cost_estimate=pl.CostEstimate(flops=6 * 10**9, bytes_accessed=20 * 10**6, transcendentals=2**18),
    )(
        tokens.reshape(4, rows // 4, depth),
        queries[0],
        cotangent[0],
        key_weight,
        value_weight,
        probe,
    )


def head_rows(block, head_index, group):
    width = group * HEAD_DIM
    return block[:, head_index * width : (head_index + 1) * width].reshape(-1, HEAD_DIM)


def forward_stats(query_rows, cot_rows, head_context, query_start, block, block_count, group):
    scaling = HEAD_DIM ** (-0.5)
    keys, values, tan_keys, tan_values = head_context
    row_count = query_rows.shape[0]
    query_pos = query_start + jnp.arange(row_count, dtype=jnp.int32) // group

    def masked_scores(block_index):
        offset = block_index * block
        key_block = lax.dynamic_slice_in_dim(keys, offset, block, 0)
        key_pos = offset + jnp.arange(block, dtype=jnp.int32)
        valid = key_pos[None, :] <= query_pos[:, None]
        return (jnp.where(valid, scaling * times_t(query_rows, key_block), NEG_FILL), offset)

    def peak_step(block_index, peak):
        scores, offset = masked_scores(block_index)
        return jnp.maximum(peak, jnp.max(scores, axis=1))

    peak = lax.fori_loop(0, block_count, peak_step, jnp.full((row_count,), NEG_FILL, jnp.float32))

    def accumulate(block_index, carry):
        total, along, acc_value, acc_mixed, acc_tan = carry
        scores, offset = masked_scores(block_index)
        tan_scores = scaling * times_t(
            query_rows, lax.dynamic_slice_in_dim(tan_keys, offset, block, 0)
        )
        value_block = lax.dynamic_slice_in_dim(values, offset, block, 0)
        tan_value_block = lax.dynamic_slice_in_dim(tan_values, offset, block, 0)
        expo = jnp.exp(scores - peak[:, None])
        expo_half = expo.astype(jnp.bfloat16)
        total = total + jnp.sum(expo, axis=1)
        along = along + jnp.sum(expo * tan_scores, axis=1)
        acc_value = acc_value + jnp.dot(expo_half, value_block, preferred_element_type=jnp.float32)
        acc_mixed = acc_mixed + jnp.dot(
            (expo * tan_scores).astype(jnp.bfloat16),
            value_block,
            preferred_element_type=jnp.float32,
        )
        acc_tan = acc_tan + jnp.dot(expo_half, tan_value_block, preferred_element_type=jnp.float32)
        return (total, along, acc_value, acc_mixed, acc_tan)

    row_zero = jnp.zeros((row_count,), jnp.float32)
    block_zero = jnp.zeros((row_count, HEAD_DIM), jnp.float32)
    total, along, acc_value, acc_mixed, acc_tan = lax.fori_loop(
        0, block_count, accumulate, (row_zero, row_zero, block_zero, block_zero, block_zero)
    )
    output = acc_value / total[:, None]
    shift_mean = along / total
    tan_output = (acc_mixed - shift_mean[:, None] * acc_value) / total[:, None] + acc_tan / total[
        :, None
    ]
    cot_float = cot_rows.astype(jnp.float32)
    delta = jnp.sum(cot_float * output, axis=1)
    tan_delta = jnp.sum(cot_float * tan_output, axis=1)
    return (peak, total, shift_mean, delta, tan_delta)


def pair_terms(query_block, cot_block, stats, query_start, kv_block, key_start, group, local_kv):
    scaling = HEAD_DIM ** (-0.5)
    query_count = query_block.shape[0]
    key_count = kv_block[0].shape[0]

    def compute():
        key_parts = []
        value_parts = []
        for head_index in range(local_kv):
            columns = slice(head_index * HEAD_DIM, (head_index + 1) * HEAD_DIM)
            keys = kv_block[0][:, columns]
            values = kv_block[1][:, columns]
            tan_keys = kv_block[2][:, columns]
            tan_values = kv_block[3][:, columns]
            query_rows = head_rows(query_block, head_index, group)
            cot_rows = head_rows(cot_block, head_index, group)
            peak, total, shift_mean, delta, tan_delta = tuple(
                (
                    item[:, head_index * group : (head_index + 1) * group].reshape(-1)
                    for item in stats
                )
            )
            query_pos = query_start + jnp.arange(query_count * group, dtype=jnp.int32) // group
            key_pos = jnp.arange(key_count, dtype=jnp.int32)
            valid = key_pos[None, :] <= query_pos[:, None]
            scores = jnp.where(valid, scaling * times_t(query_rows, keys), NEG_FILL)
            tan_scores = scaling * times_t(query_rows, tan_keys)
            probs = jnp.exp(scores - peak[:, None]) / total[:, None]
            tan_probs = probs * (tan_scores - shift_mean[:, None])
            value_parts.append(times_tn(tan_probs.astype(jnp.bfloat16), cot_rows))
            dprob = times_t(cot_rows, values)
            tan_dprob = times_t(cot_rows, tan_values)
            tan_dscore = tan_probs * (dprob - delta[:, None]) + probs * (
                tan_dprob - tan_delta[:, None]
            )
            key_parts.append(scaling * times_tn(tan_dscore.astype(jnp.bfloat16), query_rows))
        return jnp.concatenate(key_parts + value_parts, axis=1)

    def nothing():
        return jnp.zeros((key_count, 2 * local_kv * HEAD_DIM), jnp.float32)

    return lax.cond(key_start <= query_start + query_count - 1, compute, nothing)


def local(tokens, queries, cotangent, key_weight, value_weight, probe):
    tok = tokens[0]
    query_local = queries[0]
    cot_local = cotangent[0]
    tok_rows = tok.shape[0]
    model_dim = tok.shape[1]
    width = key_weight.shape[1]
    local_kv = width // HEAD_DIM
    group = HEADS // KV_HEADS
    sign = probe.astype(jnp.float32).astype(jnp.bfloat16)
    ctx_size = lax.axis_size("ctx")
    position = lax.axis_index("ctx")
    columns = tok
    sign_key = sign[0]
    sign_value = sign[1]
    projected = (
        jnp.dot(
            columns,
            lax.all_gather(key_weight, "ctx", axis=0, tiled=True),
            preferred_element_type=jnp.float32,
        ),
        jnp.dot(
            columns,
            lax.all_gather(value_weight, "ctx", axis=0, tiled=True),
            preferred_element_type=jnp.float32,
        ),
        jnp.dot(columns, sign_key, preferred_element_type=jnp.float32),
        jnp.dot(columns, sign_value, preferred_element_type=jnp.float32),
    )
    own_keys, own_values, own_tan_keys, own_tan_values = tuple(
        (item.astype(jnp.bfloat16) for item in projected)
    )
    context = (
        lax.all_gather(own_keys, "ctx", axis=0, tiled=True),
        lax.all_gather(own_values, "ctx", axis=0, tiled=True),
        lax.all_gather(own_tan_keys, "ctx", axis=0, tiled=True),
        lax.all_gather(own_tan_values, "ctx", axis=0, tiled=True),
    )
    per_block = 1
    while per_block * 2 <= max(1, 512 // tok_rows) and ctx_size % (per_block * 2) == 0:
        per_block = per_block * 2
    block = per_block * tok_rows
    query_start = position * tok_rows
    block_count = (query_start + tok_rows - 1) // block + 1
    stat_lists = ([], [], [], [], [])
    for head_index in range(local_kv):
        head_context = tuple(
            (item[:, head_index * HEAD_DIM : (head_index + 1) * HEAD_DIM] for item in context)
        )
        results = forward_stats(
            head_rows(query_local, head_index, group),
            head_rows(cot_local, head_index, group),
            head_context,
            query_start,
            block,
            block_count,
            group,
        )
        for member in range(5):
            stat_lists[member].append(results[member].reshape(tok_rows, group))
    stat_peak, stat_total, stat_shift, stat_delta, stat_tan_delta = tuple(
        (jnp.concatenate(items, axis=1) for items in stat_lists)
    )
    stats = (stat_peak, stat_total, stat_shift, stat_delta, stat_tan_delta)
    kv_block = tuple((item for item in context))
    terms = lax.psum_scatter(
        pair_terms(
            query_local, cot_local, stats, query_start, kv_block, jnp.int32(0), group, local_kv
        ),
        "ctx",
        scatter_dimension=0,
        tiled=True,
    )
    grads = terms.astype(jnp.bfloat16)
    own_rows = model_dim // ctx_size
    columns = tok
    partial_hvp = lax.psum_scatter(times_tn(columns, grads), "ctx", scatter_dimension=0, tiled=True)
    hvp = lax.psum(partial_hvp, "rep")
    hvp = hvp.reshape(own_rows, 2, width).transpose(1, 0, 2)
    sign_rows = lax.dynamic_slice_in_dim(probe, position * own_rows, own_rows, 1).astype(
        jnp.float32
    )
    return sign_rows * hvp


def fits(mesh, tokens):
    sizes = mesh.shape
    return (
        sizes["ctx"] == 2
        and sizes["head"] == 4
        and sizes["rep"] == 4
        and tokens.shape[0] == 4
        and tokens.shape[1] == 256
        and tokens.shape[2] == 4096
    )


def solution(mesh):
    def run(*arguments):
        return mapped(mesh, fused if fits(mesh, arguments[0]) else local)(*arguments)

    return run


def mapped(mesh, body):
    return jax.shard_map(
        body,
        mesh=mesh,
        in_specs=(
            P("rep", "ctx", None),
            P("rep", "ctx", "head"),
            P("rep", "ctx", "head"),
            P("ctx", "head"),
            P("ctx", "head"),
            P(None, None, "head"),
        ),
        out_specs=P(None, "ctx", "head"),
        check_vma=False,
    )
```

```python
import functools

import jax
import jax.numpy as jnp
from jax import lax
from jax.experimental import pallas as pl
from jax.experimental.pallas import tpu as pltpu
from jax.sharding import PartitionSpec as P

HEADS = 32
KV_HEADS = 8
HEAD_DIM = 128


NEG_FILL = -1e30

BF16 = jnp.bfloat16
F32 = jnp.float32
CHUNKS = 4
N_REMOTE = 40


def times_t(left, right):
    return lax.dot_general(
        left, right, (((1,), (1,)), ((), ())), preferred_element_type=jnp.float32
    )


def times_tn(left, right):
    return lax.dot_general(
        left, right, (((0,), (0,)), ((), ())), preferred_element_type=jnp.float32
    )


def fused_kernel(tok, q, cot, kw, vw, probe, out,
                 gath, toks, qs, cots, kws, vws, signs, tan_own, tan_all,
                 part_own, part_in, grads, acc,
                 send_sem, recv_sem, local_sem, probe_sem, out_sem):
    x = lax.axis_index("ctx")
    h = lax.axis_index("head")
    z = lax.axis_index("rep")
    half = gath.shape[-1]
    rows = qs.shape[1]
    other = 1 - x
    sib = h + 1 - 2 * lax.rem(h, 2)
    yn = lax.rem(h + 2, 4)
    sib_yn = lax.rem(sib + 2, 4)
    zs = (z + 1 - 2 * lax.rem(z, 2), lax.rem(z + 2, 4), 3 - z)
    to_x = (other, h, z)
    to_s = (x, sib, z)
    to_y = (x, yn, z)
    to_z = tuple((x, h, zd) for zd in zs)

    def cols(index, width):
        return pl.ds(pl.multiple_of(index * width, width), width)

    loads = [
        pltpu.make_async_copy(tok, toks, local_sem.at[0]),
        pltpu.make_async_copy(tok.at[:, :, cols(x, half)], gath.at[z, :, x], local_sem.at[1]),
        pltpu.make_async_copy(kw, kws, local_sem.at[2]),
        pltpu.make_async_copy(vw, vws, local_sem.at[3]),
        pltpu.make_async_copy(q.at[:, cols(x, 512)], qs.at[x], local_sem.at[4]),
        pltpu.make_async_copy(cot.at[:, cols(x, 512)], cots.at[x], local_sem.at[5]),
    ]
    step = 2 * half // CHUNKS
    probes = [
        [
            pltpu.make_async_copy(
                probe.at[t, pl.ds(c * step, step)],
                signs.at[t, pl.ds(c * step, step)],
                probe_sem.at[t * CHUNKS + c],
            )
            for c in range(CHUNKS)
        ]
        for t in range(2)
    ]
    for index in (0, 2, 3, 1):
        loads[index].start()
    for t in range(2):
        for c in range(CHUNKS):
            probes[t][c].start()
    for index in (4, 5):
        loads[index].start()

    barrier = pltpu.get_barrier_semaphore()
    for device in (to_x, to_s, to_y) + to_z:
        pl.semaphore_signal(barrier, inc=1, device_id=device, device_id_type=pl.DeviceIdType.MESH)
    pl.semaphore_wait(barrier, 6)

    sent = []

    def send(index, src, dst, device):
        copy = pltpu.make_async_remote_copy(
            src_ref=src, dst_ref=dst, send_sem=send_sem.at[index], recv_sem=recv_sem.at[index],
            device_id=device, device_id_type=pl.DeviceIdType.MESH,
        )
        copy.start()
        sent.append(copy)

    def arrive(index, slot, device):
        pltpu.make_async_remote_copy(
            src_ref=slot, dst_ref=slot, send_sem=send_sem.at[index], recv_sem=recv_sem.at[index],
            device_id=device, device_id_type=pl.DeviceIdType.MESH,
        ).wait_recv()

    send(0, tok.at[h, :, cols(other, half)], gath.at[z, h, x], to_x)
    for d in range(3):
        send(1 + d, tok.at[h, :, cols(x, half)], gath.at[z, h, x], to_z[d])
    send(19, q.at[:, cols(other, 512)], qs.at[x], to_x)
    send(20, cot.at[:, cols(other, 512)], cots.at[x], to_x)

    def project_tangent(t):
        total = jnp.zeros((rows, 256), F32)
        for c in range(CHUNKS):
            probes[t][c].wait()
            sign = signs[t, pl.ds(c * step, step), :].astype(F32).astype(BF16)
            block = toks[:, :, pl.ds(c * step, step)].reshape(rows, step)
            total = total + jnp.dot(block, sign, preferred_element_type=F32)
        half_total = total.astype(BF16)
        for j in range(2):
            tan_own[j, :, :, t * 128:(t + 1) * 128] = half_total[:, j * 128:(j + 1) * 128].reshape(4, rows // 4, 128)

    def project_rows(block, ctx):
        for t, weight in enumerate((kws, vws)):
            partial = jnp.dot(block.reshape(rows, half), weight[...], preferred_element_type=F32)
            for j in range(2):
                part_own[j, :, pl.ds(ctx, 1), :, t * 128:(t + 1) * 128] = (
                    partial[:, j * 128:(j + 1) * 128].reshape(4, 1, rows // 4, 128)
                )

    for index in (0, 2, 3):
        loads[index].wait()
    project_rows(toks[:, :, cols(x, half)], x)
    send(22, part_own.at[other, :, x], part_in.at[:, x], to_x)
    project_tangent(0)
    arrive(0, gath.at[z, h, other], to_x)
    send(7, gath.at[z, h, other], gath.at[z, h, other], to_y)
    send(8, gath.at[z, h, other], gath.at[z, h, other], to_s)
    for d in range(3):
        send(4 + d, gath.at[z, h, other], gath.at[z, h, other], to_z[d])
    project_tangent(1)
    send(21, tan_own.at[other], tan_all.at[:, x], to_x)
    tan_all[:, pl.ds(x, 1)] = tan_own[x][:, None]
    arrive(8, gath.at[z, sib, other], to_s)
    arrive(7, gath.at[z, yn, other], to_y)
    send(9, gath.at[z, yn, other], gath.at[z, yn, other], to_s)
    arrive(9, gath.at[z, sib_yn, other], to_s)
    seq = 2 * rows
    project_rows(gath[z, :, other], other)
    send(39, part_own.at[other, :, other], part_in.at[:, other], to_x)

    ctxs = (x, other)
    from_z = ((1, 2, 3), (4, 5, 6))
    from_y = ((10, 11, 12), (30, 31, 32))
    from_s = ((13, 14, 15), (33, 34, 35))
    from_sy = ((16, 17, 18), (36, 37, 38))

    def pass_rep(part, d):
        at = gath.at[zs[d], h, ctxs[part]]
        arrive(from_z[part][d], at, to_z[d])
        send(from_y[part][d], at, at, to_y)
        send(from_s[part][d], at, at, to_s)

    def pass_sibling(part, d):
        at = gath.at[zs[d], yn, ctxs[part]]
        arrive(from_y[part][d], at, to_y)
        send(from_sy[part][d], at, at, to_s)

    for d in range(3):
        pass_rep(0, d)
    loads[1].wait()
    loads[4].wait()
    loads[5].wait()
    arrive(19, qs.at[other], to_x)
    arrive(20, cots.at[other], to_x)
    arrive(21, tan_all.at[:, other], to_x)
    arrive(22, part_in.at[:, other], to_x)
    arrive(39, part_in.at[:, x], to_x)

    both = (part_own[x] + part_in[...]).reshape(seq, 256).astype(BF16)
    keys, values = both[:, :128], both[:, 128:]
    tangents = tan_all[...].reshape(seq, 256)
    tan_keys, tan_values = tangents[:, :128], tangents[:, 128:]
    scaling = HEAD_DIM ** (-0.5)
    quarter = rows // 4
    slot = lax.broadcasted_iota(jnp.int32, (seq, seq), 1)
    key_pos = (
        lax.rem(lax.div(slot, quarter), 2) * rows
        + lax.div(slot, 2 * quarter) * quarter
        + lax.rem(slot, quarter)
    )
    valid = key_pos <= lax.broadcasted_iota(jnp.int32, (seq, seq), 0)
    key_terms = jnp.zeros((seq, 128), F32)
    value_terms = jnp.zeros((seq, 128), F32)
    for g in range(4):
        span = slice(g * 128, (g + 1) * 128)
        query = qs[:, :, span].reshape(seq, 128)
        cotan = cots[:, :, span].reshape(seq, 128)
        scores = jnp.where(valid, scaling * times_t(query, keys), NEG_FILL)
        tan_scores = scaling * times_t(query, tan_keys)
        peak = jnp.max(scores, axis=1, keepdims=True)
        expo = jnp.exp(scores - peak)
        total = jnp.sum(expo, axis=1, keepdims=True)
        mixed = expo * tan_scores
        along = jnp.sum(mixed, axis=1, keepdims=True)
        expo_half = expo.astype(BF16)
        acc_value = jnp.dot(expo_half, values, preferred_element_type=F32)
        acc_mixed = jnp.dot(mixed.astype(BF16), values, preferred_element_type=F32)
        acc_tan = jnp.dot(expo_half, tan_values, preferred_element_type=F32)
        inverse = 1.0 / total
        shift_mean = along * inverse
        tan_sum = acc_mixed - shift_mean * acc_value + acc_tan
        cot_float = cotan.astype(F32)
        delta = jnp.sum(cot_float * acc_value, axis=1, keepdims=True) * inverse
        tan_delta = jnp.sum(cot_float * tan_sum, axis=1, keepdims=True) * inverse
        probs = expo * inverse
        tan_probs = probs * (tan_scores - shift_mean)
        dprob = times_t(cotan, values)
        tan_dprob = times_t(cotan, tan_values)
        tan_dscore = tan_probs * (dprob - delta) + probs * (tan_dprob - tan_delta)
        value_terms = value_terms + times_tn(tan_probs.astype(BF16), cotan)
        key_terms = key_terms + times_tn(tan_dscore.astype(BF16), query)
    own = cols(x, 128)
    theirs = cols(other, 128)
    grads[z, 0, :, own] = (scaling * key_terms).astype(BF16)
    grads[z, 1, :, own] = value_terms.astype(BF16)
    mine_at = grads.at[z, :, :, own]
    for d in range(3):
        send(24 + d, mine_at, mine_at, to_z[d])
    send(23, mine_at, mine_at, to_x)
    for d in range(3):
        pass_rep(1, d)
    for d in range(3):
        pass_sibling(0, d)

    block = 256
    blocks = half // block

    def product(rep, start, t):
        left = gath[rep, :, :, :, pl.ds(start, block)].reshape(seq, block)
        return times_tn(left, grads[rep, t])

    def pass_grads(d):
        at = grads.at[zs[d], :, :, own]
        arrive(24 + d, at, to_z[d])
        send(27 + d, at, at, to_x)

    def add_rep(rep, first):
        @pl.loop(0, blocks)
        def _(i):
            start = pl.multiple_of(i * block, block)
            for t in range(2):
                value = product(rep, start, t)
                if not first:
                    value = value + acc[t, pl.ds(start, block), :]
                acc[t, pl.ds(start, block), :] = value

    def rest_of(d):
        for part in range(2):
            arrive(from_s[part][d], gath.at[zs[d], sib, ctxs[part]], to_s)
            arrive(from_sy[part][d], gath.at[zs[d], sib_yn, ctxs[part]], to_s)
        arrive(27 + d, grads.at[zs[d], :, :, theirs], to_x)

    pass_grads(0)
    arrive(23, grads.at[z, :, :, theirs], to_x)
    add_rep(z, True)
    pass_grads(1)
    pass_grads(2)
    for d in range(3):
        pass_sibling(1, d)
    rest_of(0)
    add_rep(zs[0], False)
    rest_of(1)
    add_rep(zs[1], False)
    rest_of(2)

    def write(i):
        start = pl.multiple_of(i * block, block)
        return pltpu.make_async_copy(
            acc.at[:, pl.ds(start, block)], out.at[:, pl.ds(start, block)], out_sem.at[i]
        )

    @pl.loop(0, blocks)
    def _(i):
        start = pl.multiple_of(i * block, block)
        for t in range(2):
            value = product(zs[2], start, t) + acc[t, pl.ds(start, block), :]
            sign_at = pl.multiple_of(x * half + i * block, block)
            acc[t, pl.ds(start, block), :] = value * signs[t, pl.ds(sign_at, block), :].astype(F32)
        write(i).start()

    @pl.loop(0, blocks)
    def _(i):
        write(i).wait()

    for copy in sent:
        copy.wait_send()


def fused(tokens, queries, cotangent, key_weight, value_weight, probe):
    _, rows, depth = tokens.shape
    half = key_weight.shape[0]
    any_spec = pl.BlockSpec(memory_space=pl.ANY)
    return pl.pallas_call(
        fused_kernel,
        out_shape=jax.ShapeDtypeStruct((2, half, 256), F32),
        in_specs=[any_spec] * 6,
        out_specs=any_spec,
        scratch_shapes=[
            pltpu.VMEM((4, 4, 2, rows // 4, half), BF16),
            pltpu.VMEM((4, rows // 4, depth), BF16),
            pltpu.VMEM((2, rows, 512), BF16),
            pltpu.VMEM((2, rows, 512), BF16),
            pltpu.VMEM((half, 256), BF16),
            pltpu.VMEM((half, 256), BF16),
            pltpu.VMEM((2, depth, 256), jnp.int32),
            pltpu.VMEM((2, 4, rows // 4, 256), BF16),
            pltpu.VMEM((4, 2, rows // 4, 256), BF16),
            pltpu.VMEM((2, 4, 2, rows // 4, 256), F32),
            pltpu.VMEM((4, 2, rows // 4, 256), F32),
            pltpu.VMEM((4, 2, 2 * rows, 256), BF16),
            pltpu.VMEM((2, half, 256), F32),
            pltpu.SemaphoreType.DMA((N_REMOTE,)),
            pltpu.SemaphoreType.DMA((N_REMOTE,)),
            pltpu.SemaphoreType.DMA((6,)),
            pltpu.SemaphoreType.DMA((2 * CHUNKS,)),
            pltpu.SemaphoreType.DMA((half // 256,)),
        ],
        compiler_params=pltpu.CompilerParams(
            collective_id=0, has_side_effects=True, vmem_limit_bytes=56 * 1024 * 1024
        ),
        cost_estimate=pl.CostEstimate(flops=6 * 10**9, bytes_accessed=20 * 10**6, transcendentals=2**18),
    )(
        tokens.reshape(4, rows // 4, depth),
        queries[0],
        cotangent[0],
        key_weight,
        value_weight,
        probe,
    )


def head_rows(block, head_index, group):
    width = group * HEAD_DIM
    return block[:, head_index * width : (head_index + 1) * width].reshape(-1, HEAD_DIM)


def forward_stats(query_rows, cot_rows, head_context, query_start, block, block_count, group):
    scaling = HEAD_DIM ** (-0.5)
    keys, values, tan_keys, tan_values = head_context
    row_count = query_rows.shape[0]
    query_pos = query_start + jnp.arange(row_count, dtype=jnp.int32) // group

    def masked_scores(block_index):
        offset = block_index * block
        key_block = lax.dynamic_slice_in_dim(keys, offset, block, 0)
        key_pos = offset + jnp.arange(block, dtype=jnp.int32)
        valid = key_pos[None, :] <= query_pos[:, None]
        return (jnp.where(valid, scaling * times_t(query_rows, key_block), NEG_FILL), offset)

    def peak_step(block_index, peak):
        scores, offset = masked_scores(block_index)
        return jnp.maximum(peak, jnp.max(scores, axis=1))

    peak = lax.fori_loop(0, block_count, peak_step, jnp.full((row_count,), NEG_FILL, jnp.float32))

    def accumulate(block_index, carry):
        total, along, acc_value, acc_mixed, acc_tan = carry
        scores, offset = masked_scores(block_index)
        tan_scores = scaling * times_t(
            query_rows, lax.dynamic_slice_in_dim(tan_keys, offset, block, 0)
        )
        value_block = lax.dynamic_slice_in_dim(values, offset, block, 0)
        tan_value_block = lax.dynamic_slice_in_dim(tan_values, offset, block, 0)
        expo = jnp.exp(scores - peak[:, None])
        expo_half = expo.astype(jnp.bfloat16)
        total = total + jnp.sum(expo, axis=1)
        along = along + jnp.sum(expo * tan_scores, axis=1)
        acc_value = acc_value + jnp.dot(expo_half, value_block, preferred_element_type=jnp.float32)
        acc_mixed = acc_mixed + jnp.dot(
            (expo * tan_scores).astype(jnp.bfloat16),
            value_block,
            preferred_element_type=jnp.float32,
        )
        acc_tan = acc_tan + jnp.dot(expo_half, tan_value_block, preferred_element_type=jnp.float32)
        return (total, along, acc_value, acc_mixed, acc_tan)

    row_zero = jnp.zeros((row_count,), jnp.float32)
    block_zero = jnp.zeros((row_count, HEAD_DIM), jnp.float32)
    total, along, acc_value, acc_mixed, acc_tan = lax.fori_loop(
        0, block_count, accumulate, (row_zero, row_zero, block_zero, block_zero, block_zero)
    )
    output = acc_value / total[:, None]
    shift_mean = along / total
    tan_output = (acc_mixed - shift_mean[:, None] * acc_value) / total[:, None] + acc_tan / total[
        :, None
    ]
    cot_float = cot_rows.astype(jnp.float32)
    delta = jnp.sum(cot_float * output, axis=1)
    tan_delta = jnp.sum(cot_float * tan_output, axis=1)
    return (peak, total, shift_mean, delta, tan_delta)


def pair_terms(query_block, cot_block, stats, query_start, kv_block, key_start, group, local_kv):
    scaling = HEAD_DIM ** (-0.5)
    query_count = query_block.shape[0]
    key_count = kv_block[0].shape[0]

    def compute():
        key_parts = []
        value_parts = []
        for head_index in range(local_kv):
            columns = slice(head_index * HEAD_DIM, (head_index + 1) * HEAD_DIM)
            keys = kv_block[0][:, columns]
            values = kv_block[1][:, columns]
            tan_keys = kv_block[2][:, columns]
            tan_values = kv_block[3][:, columns]
            query_rows = head_rows(query_block, head_index, group)
            cot_rows = head_rows(cot_block, head_index, group)
            peak, total, shift_mean, delta, tan_delta = tuple(
                (
                    item[:, head_index * group : (head_index + 1) * group].reshape(-1)
                    for item in stats
                )
            )
            query_pos = query_start + jnp.arange(query_count * group, dtype=jnp.int32) // group
            key_pos = jnp.arange(key_count, dtype=jnp.int32)
            valid = key_pos[None, :] <= query_pos[:, None]
            scores = jnp.where(valid, scaling * times_t(query_rows, keys), NEG_FILL)
            tan_scores = scaling * times_t(query_rows, tan_keys)
            probs = jnp.exp(scores - peak[:, None]) / total[:, None]
            tan_probs = probs * (tan_scores - shift_mean[:, None])
            value_parts.append(times_tn(tan_probs.astype(jnp.bfloat16), cot_rows))
            dprob = times_t(cot_rows, values)
            tan_dprob = times_t(cot_rows, tan_values)
            tan_dscore = tan_probs * (dprob - delta[:, None]) + probs * (
                tan_dprob - tan_delta[:, None]
            )
            key_parts.append(scaling * times_tn(tan_dscore.astype(jnp.bfloat16), query_rows))
        return jnp.concatenate(key_parts + value_parts, axis=1)

    def nothing():
        return jnp.zeros((key_count, 2 * local_kv * HEAD_DIM), jnp.float32)

    return lax.cond(key_start <= query_start + query_count - 1, compute, nothing)


def local(tokens, queries, cotangent, key_weight, value_weight, probe):
    tok = tokens[0]
    query_local = queries[0]
    cot_local = cotangent[0]
    tok_rows = tok.shape[0]
    model_dim = tok.shape[1]
    width = key_weight.shape[1]
    local_kv = width // HEAD_DIM
    group = HEADS // KV_HEADS
    sign = probe.astype(jnp.float32).astype(jnp.bfloat16)
    ctx_size = lax.axis_size("ctx")
    position = lax.axis_index("ctx")
    columns = tok
    sign_key = sign[0]
    sign_value = sign[1]
    projected = (
        jnp.dot(
            columns,
            lax.all_gather(key_weight, "ctx", axis=0, tiled=True),
            preferred_element_type=jnp.float32,
        ),
        jnp.dot(
            columns,
            lax.all_gather(value_weight, "ctx", axis=0, tiled=True),
            preferred_element_type=jnp.float32,
        ),
        jnp.dot(columns, sign_key, preferred_element_type=jnp.float32),
        jnp.dot(columns, sign_value, preferred_element_type=jnp.float32),
    )
    own_keys, own_values, own_tan_keys, own_tan_values = tuple(
        (item.astype(jnp.bfloat16) for item in projected)
    )
    context = (
        lax.all_gather(own_keys, "ctx", axis=0, tiled=True),
        lax.all_gather(own_values, "ctx", axis=0, tiled=True),
        lax.all_gather(own_tan_keys, "ctx", axis=0, tiled=True),
        lax.all_gather(own_tan_values, "ctx", axis=0, tiled=True),
    )
    per_block = 1
    while per_block * 2 <= max(1, 512 // tok_rows) and ctx_size % (per_block * 2) == 0:
        per_block = per_block * 2
    block = per_block * tok_rows
    query_start = position * tok_rows
    block_count = (query_start + tok_rows - 1) // block + 1
    stat_lists = ([], [], [], [], [])
    for head_index in range(local_kv):
        head_context = tuple(
            (item[:, head_index * HEAD_DIM : (head_index + 1) * HEAD_DIM] for item in context)
        )
        results = forward_stats(
            head_rows(query_local, head_index, group),
            head_rows(cot_local, head_index, group),
            head_context,
            query_start,
            block,
            block_count,
            group,
        )
        for member in range(5):
            stat_lists[member].append(results[member].reshape(tok_rows, group))
    stat_peak, stat_total, stat_shift, stat_delta, stat_tan_delta = tuple(
        (jnp.concatenate(items, axis=1) for items in stat_lists)
    )
    stats = (stat_peak, stat_total, stat_shift, stat_delta, stat_tan_delta)
    kv_block = tuple((item for item in context))
    terms = lax.psum_scatter(
        pair_terms(
            query_local, cot_local, stats, query_start, kv_block, jnp.int32(0), group, local_kv
        ),
        "ctx",
        scatter_dimension=0,
        tiled=True,
    )
    grads = terms.astype(jnp.bfloat16)
    own_rows = model_dim // ctx_size
    columns = tok
    partial_hvp = lax.psum_scatter(times_tn(columns, grads), "ctx", scatter_dimension=0, tiled=True)
    hvp = lax.psum(partial_hvp, "rep")
    hvp = hvp.reshape(own_rows, 2, width).transpose(1, 0, 2)
    sign_rows = lax.dynamic_slice_in_dim(probe, position * own_rows, own_rows, 1).astype(
        jnp.float32
    )
    return sign_rows * hvp


def fits(mesh, tokens):
    sizes = mesh.shape
    return (
        sizes["ctx"] == 2
        and sizes["head"] == 4
        and sizes["rep"] == 4
        and tokens.shape[0] == 4
        and tokens.shape[1] == 256
        and tokens.shape[2] == 4096
    )


def solution(mesh):
    def run(*arguments):
        return mapped(mesh, fused if fits(mesh, arguments[0]) else local)(*arguments)

    return run


def mapped(mesh, body):
    return jax.shard_map(
        body,
        mesh=mesh,
        in_specs=(
            P("rep", "ctx", None),
            P("rep", "ctx", "head"),
            P("rep", "ctx", "head"),
            P("ctx", "head"),
            P("ctx", "head"),
            P(None, None, "head"),
        ),
        out_specs=P(None, "ctx", "head"),
        check_vma=False,
    )
```

```python
import functools

import jax
import jax.numpy as jnp
from jax import lax
from jax.experimental import pallas as pl
from jax.experimental.pallas import tpu as pltpu
from jax.sharding import PartitionSpec as P

HEADS = 32
KV_HEADS = 8
HEAD_DIM = 128


NEG_FILL = -1e30

BF16 = jnp.bfloat16
F32 = jnp.float32
CHUNKS = 4
N_REMOTE = 40
STORES = 8


def times_t(left, right):
    return lax.dot_general(
        left, right, (((1,), (1,)), ((), ())), preferred_element_type=jnp.float32
    )


def times_tn(left, right):
    return lax.dot_general(
        left, right, (((0,), (0,)), ((), ())), preferred_element_type=jnp.float32
    )


def fused_kernel(tok, q, cot, kw, vw, probe, acc,
                 gath, toks, qs, cots, kws, vws, signs, tan_own, tan_all,
                 part_own, part_in, grads, flipped,
                 send_sem, recv_sem, local_sem, probe_sem):
    x = lax.axis_index("ctx")
    h = lax.axis_index("head")
    z = lax.axis_index("rep")
    half = gath.shape[-1]
    rows = qs.shape[1]
    other = 1 - x
    sib = h + 1 - 2 * lax.rem(h, 2)
    yn = lax.rem(h + 2, 4)
    sib_yn = lax.rem(sib + 2, 4)
    zs = (z + 1 - 2 * lax.rem(z, 2), lax.rem(z + 2, 4), 3 - z)
    to_x = (other, h, z)
    to_s = (x, sib, z)
    to_y = (x, yn, z)
    to_z = tuple((x, h, zd) for zd in zs)

    def cols(index, width):
        return pl.ds(pl.multiple_of(index * width, width), width)

    loads = [
        pltpu.make_async_copy(tok, toks, local_sem.at[0]),
        pltpu.make_async_copy(tok.at[:, :, cols(x, half)], gath.at[z, :, x], local_sem.at[1]),
        pltpu.make_async_copy(kw, kws, local_sem.at[2]),
        pltpu.make_async_copy(vw, vws, local_sem.at[3]),
        pltpu.make_async_copy(q.at[:, cols(x, 512)], qs.at[x], local_sem.at[4]),
        pltpu.make_async_copy(cot.at[:, cols(x, 512)], cots.at[x], local_sem.at[5]),
    ]
    step = 2 * half // CHUNKS
    probes = [
        [
            pltpu.make_async_copy(
                probe.at[t, pl.ds(c * step, step)],
                signs.at[t, pl.ds(c * step, step)],
                probe_sem.at[t * CHUNKS + c],
            )
            for c in range(CHUNKS)
        ]
        for t in range(2)
    ]
    for index in (0, 2, 3, 1):
        loads[index].start()
    for t in range(2):
        for c in range(CHUNKS):
            probes[t][c].start()
    for index in (4, 5):
        loads[index].start()

    barrier = pltpu.get_barrier_semaphore()
    for device in (to_x, to_s, to_y) + to_z:
        pl.semaphore_signal(barrier, inc=1, device_id=device, device_id_type=pl.DeviceIdType.MESH)
    pl.semaphore_wait(barrier, 6)

    sent = []

    def send(index, src, dst, device):
        copy = pltpu.make_async_remote_copy(
            src_ref=src, dst_ref=dst, send_sem=send_sem.at[index], recv_sem=recv_sem.at[index],
            device_id=device, device_id_type=pl.DeviceIdType.MESH,
        )
        copy.start()
        sent.append(copy)

    def arrive(index, slot, device):
        pltpu.make_async_remote_copy(
            src_ref=slot, dst_ref=slot, send_sem=send_sem.at[index], recv_sem=recv_sem.at[index],
            device_id=device, device_id_type=pl.DeviceIdType.MESH,
        ).wait_recv()

    send(0, tok.at[h, :, cols(other, half)], gath.at[z, h, x], to_x)
    for d in range(3):
        send(1 + d, tok.at[h, :, cols(x, half)], gath.at[z, h, x], to_z[d])
    send(19, q.at[:, cols(other, 512)], qs.at[x], to_x)
    send(20, cot.at[:, cols(other, 512)], cots.at[x], to_x)

    def project_tangent(t):
        total = jnp.zeros((rows, 256), F32)
        for c in range(CHUNKS):
            probes[t][c].wait()
            sign = signs[t, pl.ds(c * step, step), :].astype(F32).astype(BF16)
            block = toks[:, :, pl.ds(c * step, step)].reshape(rows, step)
            total = total + jnp.dot(block, sign, preferred_element_type=F32)
        half_total = total.astype(BF16)
        for j in range(2):
            tan_own[j, :, :, t * 128:(t + 1) * 128] = half_total[:, j * 128:(j + 1) * 128].reshape(4, rows // 4, 128)

    def project_rows(block, ctx):
        for t, weight in enumerate((kws, vws)):
            partial = jnp.dot(block.reshape(rows, half), weight[...], preferred_element_type=F32)
            for j in range(2):
                part_own[j, :, pl.ds(ctx, 1), :, t * 128:(t + 1) * 128] = (
                    partial[:, j * 128:(j + 1) * 128].reshape(4, 1, rows // 4, 128)
                )

    for index in (0, 2, 3):
        loads[index].wait()
    project_rows(toks[:, :, cols(x, half)], x)
    send(22, part_own.at[other, :, x], part_in.at[:, x], to_x)
    project_tangent(0)
    arrive(0, gath.at[z, h, other], to_x)
    send(7, gath.at[z, h, other], gath.at[z, h, other], to_y)
    send(8, gath.at[z, h, other], gath.at[z, h, other], to_s)
    for d in range(3):
        send(4 + d, gath.at[z, h, other], gath.at[z, h, other], to_z[d])
    project_tangent(1)
    send(21, tan_own.at[other], tan_all.at[:, x], to_x)
    tan_all[:, pl.ds(x, 1)] = tan_own[x][:, None]
    arrive(8, gath.at[z, sib, other], to_s)
    arrive(7, gath.at[z, yn, other], to_y)
    send(9, gath.at[z, yn, other], gath.at[z, yn, other], to_s)
    arrive(9, gath.at[z, sib_yn, other], to_s)
    seq = 2 * rows
    project_rows(gath[z, :, other], other)
    send(39, part_own.at[other, :, other], part_in.at[:, other], to_x)

    ctxs = (x, other)
    from_z = ((1, 2, 3), (4, 5, 6))
    from_y = ((10, 11, 12), (30, 31, 32))
    from_s = ((13, 14, 15), (33, 34, 35))
    from_sy = ((16, 17, 18), (36, 37, 38))

    def pass_rep(part, d):
        at = gath.at[zs[d], h, ctxs[part]]
        arrive(from_z[part][d], at, to_z[d])
        send(from_y[part][d], at, at, to_y)
        send(from_s[part][d], at, at, to_s)

    def pass_sibling(part, d):
        at = gath.at[zs[d], yn, ctxs[part]]
        arrive(from_y[part][d], at, to_y)
        send(from_sy[part][d], at, at, to_s)

    block = 256
    blocks = half // block

    def flip(rep):
        @pl.loop(0, blocks)
        def _(i):
            start = pl.multiple_of(i * block, block)
            left = gath[rep, :, :, :, pl.ds(start, block)].reshape(seq, block)
            flipped[rep, pl.ds(start, block), :] = left.T

    for d in range(3):
        pass_rep(0, d)
    loads[1].wait()
    flip(z)
    loads[4].wait()
    loads[5].wait()
    arrive(19, qs.at[other], to_x)
    arrive(20, cots.at[other], to_x)
    arrive(21, tan_all.at[:, other], to_x)
    arrive(22, part_in.at[:, other], to_x)
    arrive(39, part_in.at[:, x], to_x)

    both = (part_own[x] + part_in[...]).reshape(seq, 256).astype(BF16)
    keys, values = both[:, :128], both[:, 128:]
    tangents = tan_all[...].reshape(seq, 256)
    tan_keys, tan_values = tangents[:, :128], tangents[:, 128:]
    scaling = HEAD_DIM ** (-0.5)
    quarter = rows // 4
    slot = lax.broadcasted_iota(jnp.int32, (seq, seq), 1)
    key_pos = (
        lax.rem(lax.div(slot, quarter), 2) * rows
        + lax.div(slot, 2 * quarter) * quarter
        + lax.rem(slot, quarter)
    )
    valid = key_pos <= lax.broadcasted_iota(jnp.int32, (seq, seq), 0)
    key_terms = jnp.zeros((seq, 128), F32)
    value_terms = jnp.zeros((seq, 128), F32)
    for g in range(4):
        span = slice(g * 128, (g + 1) * 128)
        query = qs[:, :, span].reshape(seq, 128)
        cotan = cots[:, :, span].reshape(seq, 128)
        scores = jnp.where(valid, scaling * times_t(query, keys), NEG_FILL)
        tan_scores = scaling * times_t(query, tan_keys)
        peak = jnp.max(scores, axis=1, keepdims=True)
        expo = jnp.exp(scores - peak)
        total = jnp.sum(expo, axis=1, keepdims=True)
        mixed = expo * tan_scores
        along = jnp.sum(mixed, axis=1, keepdims=True)
        expo_half = expo.astype(BF16)
        acc_value = jnp.dot(expo_half, values, preferred_element_type=F32)
        acc_mixed = jnp.dot(mixed.astype(BF16), values, preferred_element_type=F32)
        acc_tan = jnp.dot(expo_half, tan_values, preferred_element_type=F32)
        inverse = 1.0 / total
        shift_mean = along * inverse
        tan_sum = acc_mixed - shift_mean * acc_value + acc_tan
        cot_float = cotan.astype(F32)
        delta = jnp.sum(cot_float * acc_value, axis=1, keepdims=True) * inverse
        tan_delta = jnp.sum(cot_float * tan_sum, axis=1, keepdims=True) * inverse
        probs = expo * inverse
        tan_probs = probs * (tan_scores - shift_mean)
        dprob = times_t(cotan, values)
        tan_dprob = times_t(cotan, tan_values)
        tan_dscore = tan_probs * (dprob - delta) + probs * (tan_dprob - tan_delta)
        value_terms = value_terms + times_tn(tan_probs.astype(BF16), cotan)
        key_terms = key_terms + times_tn(tan_dscore.astype(BF16), query)
    own = cols(x, 128)
    theirs = cols(other, 128)
    grads[z, 0, :, own] = (scaling * key_terms).astype(BF16)
    grads[z, 1, :, own] = value_terms.astype(BF16)
    mine_at = grads.at[z, :, :, own]
    for d in range(3):
        send(24 + d, mine_at, mine_at, to_z[d])
    send(23, mine_at, mine_at, to_x)
    for d in range(3):
        pass_rep(1, d)
    for d in range(3):
        pass_sibling(0, d)

    def product(rep, start, t):
        return jnp.dot(flipped[rep, pl.ds(start, block), :], grads[rep, t], preferred_element_type=F32)

    def pass_grads(d):
        at = grads.at[zs[d], :, :, own]
        arrive(24 + d, at, to_z[d])
        send(27 + d, at, at, to_x)

    def add_rep(rep, first):
        @pl.loop(0, blocks)
        def _(i):
            start = pl.multiple_of(i * block, block)
            for t in range(2):
                value = product(rep, start, t)
                if not first:
                    value = value + acc[t, pl.ds(start, block), :]
                acc[t, pl.ds(start, block), :] = value

    def flip_rest(d):
        for part in range(2):
            arrive(from_s[part][d], gath.at[zs[d], sib, ctxs[part]], to_s)
            arrive(from_sy[part][d], gath.at[zs[d], sib_yn, ctxs[part]], to_s)
        flip(zs[d])

    pass_grads(0)
    arrive(23, grads.at[z, :, :, theirs], to_x)
    add_rep(z, True)
    for d in range(3):
        pass_sibling(1, d)
    pass_grads(1)
    flip_rest(0)
    pass_grads(2)
    flip_rest(1)
    flip_rest(2)
    arrive(27, grads.at[zs[0], :, :, theirs], to_x)
    add_rep(zs[0], False)
    arrive(28, grads.at[zs[1], :, :, theirs], to_x)
    add_rep(zs[1], False)
    arrive(29, grads.at[zs[2], :, :, theirs], to_x)

    @pl.loop(0, blocks)
    def _(i):
        start = pl.multiple_of(i * block, block)
        for t in range(2):
            value = product(zs[2], start, t) + acc[t, pl.ds(start, block), :]
            sign_at = pl.multiple_of(x * half + i * block, block)
            acc[t, pl.ds(start, block), :] = value * signs[t, pl.ds(sign_at, block), :].astype(F32)

    for copy in sent:
        copy.wait_send()


def store_kernel(result, out, sem):
    piece = result.shape[1] // STORES
    copies = [
        pltpu.make_async_copy(
            result.at[:, pl.ds(i * piece, piece)], out.at[:, pl.ds(i * piece, piece)], sem.at[i]
        )
        for i in range(STORES)
    ]
    for copy in copies:
        copy.start()
    for copy in copies:
        copy.wait()


def fused(tokens, queries, cotangent, key_weight, value_weight, probe):
    _, rows, depth = tokens.shape
    half = key_weight.shape[0]
    any_spec = pl.BlockSpec(memory_space=pl.ANY)
    result = pl.pallas_call(
        fused_kernel,
        out_shape=pltpu.VMEM((2, half, 256), F32),
        in_specs=[any_spec] * 6,
        out_specs=pl.BlockSpec(memory_space=pltpu.VMEM),
        scratch_shapes=[
            pltpu.VMEM((4, 4, 2, rows // 4, half), BF16),
            pltpu.VMEM((4, rows // 4, depth), BF16),
            pltpu.VMEM((2, rows, 512), BF16),
            pltpu.VMEM((2, rows, 512), BF16),
            pltpu.VMEM((half, 256), BF16),
            pltpu.VMEM((half, 256), BF16),
            pltpu.VMEM((2, depth, 256), jnp.int32),
            pltpu.VMEM((2, 4, rows // 4, 256), BF16),
            pltpu.VMEM((4, 2, rows // 4, 256), BF16),
            pltpu.VMEM((2, 4, 2, rows // 4, 256), F32),
            pltpu.VMEM((4, 2, rows // 4, 256), F32),
            pltpu.VMEM((4, 2, 2 * rows, 256), BF16),
            pltpu.VMEM((4, half, 2 * rows), BF16),
            pltpu.SemaphoreType.DMA((N_REMOTE,)),
            pltpu.SemaphoreType.DMA((N_REMOTE,)),
            pltpu.SemaphoreType.DMA((6,)),
            pltpu.SemaphoreType.DMA((2 * CHUNKS,)),
        ],
        compiler_params=pltpu.CompilerParams(
            collective_id=0, has_side_effects=True, vmem_limit_bytes=56 * 1024 * 1024
        ),
        cost_estimate=pl.CostEstimate(flops=6 * 10**9, bytes_accessed=20 * 10**6, transcendentals=2**18),
    )(
        pltpu.with_memory_space_constraint(tokens.reshape(4, rows // 4, depth), pltpu.HBM),
        pltpu.with_memory_space_constraint(queries[0], pltpu.HBM),
        pltpu.with_memory_space_constraint(cotangent[0], pltpu.HBM),
        pltpu.with_memory_space_constraint(key_weight, pltpu.HBM),
        pltpu.with_memory_space_constraint(value_weight, pltpu.HBM),
        probe,
    )
    return pl.pallas_call(
        store_kernel,
        out_shape=jax.ShapeDtypeStruct(result.shape, F32),
        in_specs=[pl.BlockSpec(memory_space=pltpu.VMEM)],
        out_specs=any_spec,
        scratch_shapes=[pltpu.SemaphoreType.DMA((STORES,))],
        compiler_params=pltpu.CompilerParams(vmem_limit_bytes=4 * 1024 * 1024),
        cost_estimate=pl.CostEstimate(flops=0, bytes_accessed=8 * 10**6, transcendentals=0),
    )(result)


def head_rows(block, head_index, group):
    width = group * HEAD_DIM
    return block[:, head_index * width : (head_index + 1) * width].reshape(-1, HEAD_DIM)


def forward_stats(query_rows, cot_rows, head_context, query_start, block, block_count, group):
    scaling = HEAD_DIM ** (-0.5)
    keys, values, tan_keys, tan_values = head_context
    row_count = query_rows.shape[0]
    query_pos = query_start + jnp.arange(row_count, dtype=jnp.int32) // group

    def masked_scores(block_index):
        offset = block_index * block
        key_block = lax.dynamic_slice_in_dim(keys, offset, block, 0)
        key_pos = offset + jnp.arange(block, dtype=jnp.int32)
        valid = key_pos[None, :] <= query_pos[:, None]
        return (jnp.where(valid, scaling * times_t(query_rows, key_block), NEG_FILL), offset)

    def peak_step(block_index, peak):
        scores, offset = masked_scores(block_index)
        return jnp.maximum(peak, jnp.max(scores, axis=1))

    peak = lax.fori_loop(0, block_count, peak_step, jnp.full((row_count,), NEG_FILL, jnp.float32))

    def accumulate(block_index, carry):
        total, along, acc_value, acc_mixed, acc_tan = carry
        scores, offset = masked_scores(block_index)
        tan_scores = scaling * times_t(
            query_rows, lax.dynamic_slice_in_dim(tan_keys, offset, block, 0)
        )
        value_block = lax.dynamic_slice_in_dim(values, offset, block, 0)
        tan_value_block = lax.dynamic_slice_in_dim(tan_values, offset, block, 0)
        expo = jnp.exp(scores - peak[:, None])
        expo_half = expo.astype(jnp.bfloat16)
        total = total + jnp.sum(expo, axis=1)
        along = along + jnp.sum(expo * tan_scores, axis=1)
        acc_value = acc_value + jnp.dot(expo_half, value_block, preferred_element_type=jnp.float32)
        acc_mixed = acc_mixed + jnp.dot(
            (expo * tan_scores).astype(jnp.bfloat16),
            value_block,
            preferred_element_type=jnp.float32,
        )
        acc_tan = acc_tan + jnp.dot(expo_half, tan_value_block, preferred_element_type=jnp.float32)
        return (total, along, acc_value, acc_mixed, acc_tan)

    row_zero = jnp.zeros((row_count,), jnp.float32)
    block_zero = jnp.zeros((row_count, HEAD_DIM), jnp.float32)
    total, along, acc_value, acc_mixed, acc_tan = lax.fori_loop(
        0, block_count, accumulate, (row_zero, row_zero, block_zero, block_zero, block_zero)
    )
    output = acc_value / total[:, None]
    shift_mean = along / total
    tan_output = (acc_mixed - shift_mean[:, None] * acc_value) / total[:, None] + acc_tan / total[
        :, None
    ]
    cot_float = cot_rows.astype(jnp.float32)
    delta = jnp.sum(cot_float * output, axis=1)
    tan_delta = jnp.sum(cot_float * tan_output, axis=1)
    return (peak, total, shift_mean, delta, tan_delta)


def pair_terms(query_block, cot_block, stats, query_start, kv_block, key_start, group, local_kv):
    scaling = HEAD_DIM ** (-0.5)
    query_count = query_block.shape[0]
    key_count = kv_block[0].shape[0]

    def compute():
        key_parts = []
        value_parts = []
        for head_index in range(local_kv):
            columns = slice(head_index * HEAD_DIM, (head_index + 1) * HEAD_DIM)
            keys = kv_block[0][:, columns]
            values = kv_block[1][:, columns]
            tan_keys = kv_block[2][:, columns]
            tan_values = kv_block[3][:, columns]
            query_rows = head_rows(query_block, head_index, group)
            cot_rows = head_rows(cot_block, head_index, group)
            peak, total, shift_mean, delta, tan_delta = tuple(
                (
                    item[:, head_index * group : (head_index + 1) * group].reshape(-1)
                    for item in stats
                )
            )
            query_pos = query_start + jnp.arange(query_count * group, dtype=jnp.int32) // group
            key_pos = jnp.arange(key_count, dtype=jnp.int32)
            valid = key_pos[None, :] <= query_pos[:, None]
            scores = jnp.where(valid, scaling * times_t(query_rows, keys), NEG_FILL)
            tan_scores = scaling * times_t(query_rows, tan_keys)
            probs = jnp.exp(scores - peak[:, None]) / total[:, None]
            tan_probs = probs * (tan_scores - shift_mean[:, None])
            value_parts.append(times_tn(tan_probs.astype(jnp.bfloat16), cot_rows))
            dprob = times_t(cot_rows, values)
            tan_dprob = times_t(cot_rows, tan_values)
            tan_dscore = tan_probs * (dprob - delta[:, None]) + probs * (
                tan_dprob - tan_delta[:, None]
            )
            key_parts.append(scaling * times_tn(tan_dscore.astype(jnp.bfloat16), query_rows))
        return jnp.concatenate(key_parts + value_parts, axis=1)

    def nothing():
        return jnp.zeros((key_count, 2 * local_kv * HEAD_DIM), jnp.float32)

    return lax.cond(key_start <= query_start + query_count - 1, compute, nothing)


def local(tokens, queries, cotangent, key_weight, value_weight, probe):
    tok = tokens[0]
    query_local = queries[0]
    cot_local = cotangent[0]
    tok_rows = tok.shape[0]
    model_dim = tok.shape[1]
    width = key_weight.shape[1]
    local_kv = width // HEAD_DIM
    group = HEADS // KV_HEADS
    sign = probe.astype(jnp.float32).astype(jnp.bfloat16)
    ctx_size = lax.axis_size("ctx")
    position = lax.axis_index("ctx")
    columns = tok
    sign_key = sign[0]
    sign_value = sign[1]
    projected = (
        jnp.dot(
            columns,
            lax.all_gather(key_weight, "ctx", axis=0, tiled=True),
            preferred_element_type=jnp.float32,
        ),
        jnp.dot(
            columns,
            lax.all_gather(value_weight, "ctx", axis=0, tiled=True),
            preferred_element_type=jnp.float32,
        ),
        jnp.dot(columns, sign_key, preferred_element_type=jnp.float32),
        jnp.dot(columns, sign_value, preferred_element_type=jnp.float32),
    )
    own_keys, own_values, own_tan_keys, own_tan_values = tuple(
        (item.astype(jnp.bfloat16) for item in projected)
    )
    context = (
        lax.all_gather(own_keys, "ctx", axis=0, tiled=True),
        lax.all_gather(own_values, "ctx", axis=0, tiled=True),
        lax.all_gather(own_tan_keys, "ctx", axis=0, tiled=True),
        lax.all_gather(own_tan_values, "ctx", axis=0, tiled=True),
    )
    per_block = 1
    while per_block * 2 <= max(1, 512 // tok_rows) and ctx_size % (per_block * 2) == 0:
        per_block = per_block * 2
    block = per_block * tok_rows
    query_start = position * tok_rows
    block_count = (query_start + tok_rows - 1) // block + 1
    stat_lists = ([], [], [], [], [])
    for head_index in range(local_kv):
        head_context = tuple(
            (item[:, head_index * HEAD_DIM : (head_index + 1) * HEAD_DIM] for item in context)
        )
        results = forward_stats(
            head_rows(query_local, head_index, group),
            head_rows(cot_local, head_index, group),
            head_context,
            query_start,
            block,
            block_count,
            group,
        )
        for member in range(5):
            stat_lists[member].append(results[member].reshape(tok_rows, group))
    stat_peak, stat_total, stat_shift, stat_delta, stat_tan_delta = tuple(
        (jnp.concatenate(items, axis=1) for items in stat_lists)
    )
    stats = (stat_peak, stat_total, stat_shift, stat_delta, stat_tan_delta)
    kv_block = tuple((item for item in context))
    terms = lax.psum_scatter(
        pair_terms(
            query_local, cot_local, stats, query_start, kv_block, jnp.int32(0), group, local_kv
        ),
        "ctx",
        scatter_dimension=0,
        tiled=True,
    )
    grads = terms.astype(jnp.bfloat16)
    own_rows = model_dim // ctx_size
    columns = tok
    partial_hvp = lax.psum_scatter(times_tn(columns, grads), "ctx", scatter_dimension=0, tiled=True)
    hvp = lax.psum(partial_hvp, "rep")
    hvp = hvp.reshape(own_rows, 2, width).transpose(1, 0, 2)
    sign_rows = lax.dynamic_slice_in_dim(probe, position * own_rows, own_rows, 1).astype(
        jnp.float32
    )
    return sign_rows * hvp


def fits(mesh, tokens):
    sizes = mesh.shape
    return (
        sizes["ctx"] == 2
        and sizes["head"] == 4
        and sizes["rep"] == 4
        and tokens.shape[0] == 4
        and tokens.shape[1] == 256
        and tokens.shape[2] == 4096
    )


def solution(mesh):
    def run(*arguments):
        return mapped(mesh, fused if fits(mesh, arguments[0]) else local)(*arguments)

    return run


def mapped(mesh, body):
    return jax.shard_map(
        body,
        mesh=mesh,
        in_specs=(
            P("rep", "ctx", None),
            P("rep", "ctx", "head"),
            P("rep", "ctx", "head"),
            P("ctx", "head"),
            P("ctx", "head"),
            P(None, None, "head"),
        ),
        out_specs=P(None, "ctx", "head"),
        check_vma=False,
    )
```

```python
import functools

import jax
import jax.numpy as jnp
from jax import lax
from jax.experimental import pallas as pl
from jax.experimental.pallas import tpu as pltpu
from jax.sharding import PartitionSpec as P

HEADS = 32
KV_HEADS = 8
HEAD_DIM = 128


NEG_FILL = -1e30

BF16 = jnp.bfloat16
F32 = jnp.float32
CHUNKS = 4
N_REMOTE = 43
STORES = 8


def times_t(left, right):
    return lax.dot_general(
        left, right, (((1,), (1,)), ((), ())), preferred_element_type=jnp.float32
    )


def times_tn(left, right):
    return lax.dot_general(
        left, right, (((0,), (0,)), ((), ())), preferred_element_type=jnp.float32
    )


def fused_kernel(tok, q, cot, kw, vw, probe, acc,
                 gath, toks, qs, cots, kws, vws, signs, tan_own, tan_all,
                 part_own, part_in, grads, flipped,
                 send_sem, recv_sem, local_sem, probe_sem):
    x = lax.axis_index("ctx")
    h = lax.axis_index("head")
    z = lax.axis_index("rep")
    half = gath.shape[-1]
    rows = qs.shape[1]
    other = 1 - x
    sib = h + 1 - 2 * lax.rem(h, 2)
    yn = lax.rem(h + 2, 4)
    sib_yn = lax.rem(sib + 2, 4)
    zs = (z + 1 - 2 * lax.rem(z, 2), lax.rem(z + 2, 4), 3 - z)
    to_x = (other, h, z)
    to_s = (x, sib, z)
    to_y = (x, yn, z)
    to_z = tuple((x, h, zd) for zd in zs)

    def cols(index, width):
        return pl.ds(pl.multiple_of(index * width, width), width)

    loads = [
        pltpu.make_async_copy(tok, toks, local_sem.at[0]),
        pltpu.make_async_copy(tok.at[:, :, cols(x, half)], gath.at[z, :, x], local_sem.at[1]),
        pltpu.make_async_copy(kw, kws, local_sem.at[2]),
        pltpu.make_async_copy(vw, vws, local_sem.at[3]),
        pltpu.make_async_copy(q.at[:, cols(x, 512)], qs.at[x], local_sem.at[4]),
        pltpu.make_async_copy(cot.at[:, cols(x, 512)], cots.at[x], local_sem.at[5]),
    ]
    step = 2 * half // CHUNKS
    probes = [
        [
            pltpu.make_async_copy(
                probe.at[t, pl.ds(c * step, step)],
                signs.at[t, pl.ds(c * step, step)],
                probe_sem.at[t * CHUNKS + c],
            )
            for c in range(CHUNKS)
        ]
        for t in range(2)
    ]
    for index in (0, 2, 3, 1):
        loads[index].start()
    for t in range(2):
        for c in range(CHUNKS):
            probes[t][c].start()
    for index in (4, 5):
        loads[index].start()

    barrier = pltpu.get_barrier_semaphore()
    for device in (to_x, to_s, to_y) + to_z:
        pl.semaphore_signal(barrier, inc=1, device_id=device, device_id_type=pl.DeviceIdType.MESH)
    pl.semaphore_wait(barrier, 6)
    inner = (z - 1) * (z - 2) == 0

    sent = []
    sent_inner = []

    def describe(index, src, dst, device, land=None):
        return pltpu.make_async_remote_copy(
            src_ref=src, dst_ref=dst, send_sem=send_sem.at[index],
            recv_sem=recv_sem.at[index if land is None else land],
            device_id=device, device_id_type=pl.DeviceIdType.MESH,
        )

    def send_all(*arguments):
        describe(*arguments).start()
        sent.append(arguments)

    def send_inner(*arguments):
        sent_inner.append(arguments)

        @pl.when(inner)
        def _():
            describe(*arguments).start()

    def send_rep(first, src, dst):
        send_all(first + 1, src, dst, to_z[1])
        send_inner(first + 2, src, dst, to_z[2])
        send_all(first, src, dst, to_z[0])

    def relay(index, at, land):
        send_inner(index, at, at, to_z[0], land)

    def arrive(index, slot, device):
        pltpu.make_async_remote_copy(
            src_ref=slot, dst_ref=slot, send_sem=send_sem.at[index], recv_sem=recv_sem.at[index],
            device_id=device, device_id_type=pl.DeviceIdType.MESH,
        ).wait_recv()

    send_all(0, tok.at[h, :, cols(other, half)], gath.at[z, h, x], to_x)
    send_rep(1, tok.at[h, :, cols(x, half)], gath.at[z, h, x])
    send_all(19, q.at[:, cols(other, 512)], qs.at[x], to_x)
    send_all(20, cot.at[:, cols(other, 512)], cots.at[x], to_x)

    def project_tangent(t):
        total = jnp.zeros((rows, 256), F32)
        for c in range(CHUNKS):
            probes[t][c].wait()
            sign = signs[t, pl.ds(c * step, step), :].astype(F32).astype(BF16)
            block = toks[:, :, pl.ds(c * step, step)].reshape(rows, step)
            total = total + jnp.dot(block, sign, preferred_element_type=F32)
        half_total = total.astype(BF16)
        for j in range(2):
            tan_own[j, :, :, t * 128:(t + 1) * 128] = half_total[:, j * 128:(j + 1) * 128].reshape(4, rows // 4, 128)

    def project_rows(block, ctx):
        for t, weight in enumerate((kws, vws)):
            partial = jnp.dot(block.reshape(rows, half), weight[...], preferred_element_type=F32)
            for j in range(2):
                part_own[j, :, pl.ds(ctx, 1), :, t * 128:(t + 1) * 128] = (
                    partial[:, j * 128:(j + 1) * 128].reshape(4, 1, rows // 4, 128)
                )

    for index in (0, 2, 3):
        loads[index].wait()
    project_rows(toks[:, :, cols(x, half)], x)
    send_all(22, part_own.at[other, :, x], part_in.at[:, x], to_x)
    project_tangent(0)
    arrive(0, gath.at[z, h, other], to_x)
    send_all(7, gath.at[z, h, other], gath.at[z, h, other], to_y)
    send_all(8, gath.at[z, h, other], gath.at[z, h, other], to_s)
    send_rep(4, gath.at[z, h, other], gath.at[z, h, other])
    project_tangent(1)
    send_all(21, tan_own.at[other], tan_all.at[:, x], to_x)
    tan_all[:, pl.ds(x, 1)] = tan_own[x][:, None]
    arrive(8, gath.at[z, sib, other], to_s)
    arrive(7, gath.at[z, yn, other], to_y)
    send_all(9, gath.at[z, yn, other], gath.at[z, yn, other], to_s)
    arrive(9, gath.at[z, sib_yn, other], to_s)
    seq = 2 * rows
    project_rows(gath[z, :, other], other)
    send_all(39, part_own.at[other, :, other], part_in.at[:, other], to_x)

    ctxs = (x, other)
    from_z = ((1, 2, 3), (4, 5, 6))
    from_y = ((10, 11, 12), (30, 31, 32))
    from_s = ((13, 14, 15), (33, 34, 35))
    from_sy = ((16, 17, 18), (36, 37, 38))

    def pass_rep(part, d):
        at = gath.at[zs[d], h, ctxs[part]]
        arrive(from_z[part][d], at, to_z[d])
        if d == 1:
            relay(40 + part, at, from_z[part][2])
        send_all(from_y[part][d], at, at, to_y)
        send_all(from_s[part][d], at, at, to_s)

    def pass_sibling(part, d):
        at = gath.at[zs[d], yn, ctxs[part]]
        arrive(from_y[part][d], at, to_y)
        send_all(from_sy[part][d], at, at, to_s)

    block = 256
    blocks = half // block

    def flip(rep):
        @pl.loop(0, blocks)
        def _(i):
            start = pl.multiple_of(i * block, block)
            left = gath[rep, :, :, :, pl.ds(start, block)].reshape(seq, block)
            flipped[rep, pl.ds(start, block), :] = left.T

    for d in (1, 0, 2):
        pass_rep(0, d)
    loads[1].wait()
    flip(z)
    loads[4].wait()
    loads[5].wait()
    arrive(19, qs.at[other], to_x)
    arrive(20, cots.at[other], to_x)
    arrive(21, tan_all.at[:, other], to_x)
    arrive(22, part_in.at[:, other], to_x)
    arrive(39, part_in.at[:, x], to_x)

    both = (part_own[x] + part_in[...]).reshape(seq, 256).astype(BF16)
    keys, values = both[:, :128], both[:, 128:]
    tangents = tan_all[...].reshape(seq, 256)
    tan_keys, tan_values = tangents[:, :128], tangents[:, 128:]
    scaling = HEAD_DIM ** (-0.5)
    quarter = rows // 4
    slot = lax.broadcasted_iota(jnp.int32, (seq, seq), 1)
    key_pos = (
        lax.rem(lax.div(slot, quarter), 2) * rows
        + lax.div(slot, 2 * quarter) * quarter
        + lax.rem(slot, quarter)
    )
    valid = key_pos <= lax.broadcasted_iota(jnp.int32, (seq, seq), 0)
    key_terms = jnp.zeros((seq, 128), F32)
    value_terms = jnp.zeros((seq, 128), F32)
    for g in range(4):
        if g:
            pass_rep(1, (1, 0, 2)[g - 1])
        span = slice(g * 128, (g + 1) * 128)
        query = qs[:, :, span].reshape(seq, 128)
        cotan = cots[:, :, span].reshape(seq, 128)
        scores = jnp.where(valid, scaling * times_t(query, keys), NEG_FILL)
        tan_scores = scaling * times_t(query, tan_keys)
        peak = jnp.max(scores, axis=1, keepdims=True)
        expo = jnp.exp(scores - peak)
        total = jnp.sum(expo, axis=1, keepdims=True)
        mixed = expo * tan_scores
        along = jnp.sum(mixed, axis=1, keepdims=True)
        expo_half = expo.astype(BF16)
        acc_value = jnp.dot(expo_half, values, preferred_element_type=F32)
        acc_mixed = jnp.dot(mixed.astype(BF16), values, preferred_element_type=F32)
        acc_tan = jnp.dot(expo_half, tan_values, preferred_element_type=F32)
        inverse = 1.0 / total
        shift_mean = along * inverse
        tan_sum = acc_mixed - shift_mean * acc_value + acc_tan
        cot_float = cotan.astype(F32)
        delta = jnp.sum(cot_float * acc_value, axis=1, keepdims=True) * inverse
        tan_delta = jnp.sum(cot_float * tan_sum, axis=1, keepdims=True) * inverse
        probs = expo * inverse
        tan_probs = probs * (tan_scores - shift_mean)
        dprob = times_t(cotan, values)
        tan_dprob = times_t(cotan, tan_values)
        tan_dscore = tan_probs * (dprob - delta) + probs * (tan_dprob - tan_delta)
        value_terms = value_terms + times_tn(tan_probs.astype(BF16), cotan)
        key_terms = key_terms + times_tn(tan_dscore.astype(BF16), query)
    own = cols(x, 128)
    theirs = cols(other, 128)
    grads[z, 0, :, own] = (scaling * key_terms).astype(BF16)
    grads[z, 1, :, own] = value_terms.astype(BF16)
    mine_at = grads.at[z, :, :, own]
    send_rep(24, mine_at, mine_at)
    send_all(23, mine_at, mine_at, to_x)
    for d in range(3):
        pass_sibling(0, d)

    def product(rep, start, t):
        return jnp.dot(flipped[rep, pl.ds(start, block), :], grads[rep, t], preferred_element_type=F32)

    def pass_grads(d):
        at = grads.at[zs[d], :, :, own]
        arrive(24 + d, at, to_z[d])
        if d == 1:
            relay(42, at, 26)
        send_all(27 + d, at, at, to_x)

    def add_rep(rep, first):
        @pl.loop(0, blocks)
        def _(i):
            start = pl.multiple_of(i * block, block)
            for t in range(2):
                value = product(rep, start, t)
                if not first:
                    value = value + acc[t, pl.ds(start, block), :]
                acc[t, pl.ds(start, block), :] = value

    def flip_rest(d):
        for part in range(2):
            arrive(from_s[part][d], gath.at[zs[d], sib, ctxs[part]], to_s)
            arrive(from_sy[part][d], gath.at[zs[d], sib_yn, ctxs[part]], to_s)
        flip(zs[d])

    pass_grads(1)
    arrive(23, grads.at[z, :, :, theirs], to_x)
    pass_grads(0)
    add_rep(z, True)
    for d in (1, 0, 2):
        pass_sibling(1, d)
    flip_rest(1)
    pass_grads(2)
    flip_rest(0)
    flip_rest(2)
    arrive(27, grads.at[zs[0], :, :, theirs], to_x)
    add_rep(zs[0], False)
    arrive(28, grads.at[zs[1], :, :, theirs], to_x)
    add_rep(zs[1], False)
    arrive(29, grads.at[zs[2], :, :, theirs], to_x)

    @pl.loop(0, blocks)
    def _(i):
        start = pl.multiple_of(i * block, block)
        for t in range(2):
            value = product(zs[2], start, t) + acc[t, pl.ds(start, block), :]
            sign_at = pl.multiple_of(x * half + i * block, block)
            acc[t, pl.ds(start, block), :] = value * signs[t, pl.ds(sign_at, block), :].astype(F32)

    for arguments in sent:
        describe(*arguments).wait_send()

    @pl.when(inner)
    def _():
        for arguments in sent_inner:
            describe(*arguments).wait_send()


def store_kernel(result, out, sem):
    piece = result.shape[1] // STORES
    copies = [
        pltpu.make_async_copy(
            result.at[:, pl.ds(i * piece, piece)], out.at[:, pl.ds(i * piece, piece)], sem.at[i]
        )
        for i in range(STORES)
    ]
    for copy in copies:
        copy.start()
    for copy in copies:
        copy.wait()


def fused(tokens, queries, cotangent, key_weight, value_weight, probe):
    _, rows, depth = tokens.shape
    half = key_weight.shape[0]
    any_spec = pl.BlockSpec(memory_space=pl.ANY)
    result = pl.pallas_call(
        fused_kernel,
        out_shape=pltpu.VMEM((2, half, 256), F32),
        in_specs=[any_spec] * 6,
        out_specs=pl.BlockSpec(memory_space=pltpu.VMEM),
        scratch_shapes=[
            pltpu.VMEM((4, 4, 2, rows // 4, half), BF16),
            pltpu.VMEM((4, rows // 4, depth), BF16),
            pltpu.VMEM((2, rows, 512), BF16),
            pltpu.VMEM((2, rows, 512), BF16),
            pltpu.VMEM((half, 256), BF16),
            pltpu.VMEM((half, 256), BF16),
            pltpu.VMEM((2, depth, 256), jnp.int32),
            pltpu.VMEM((2, 4, rows // 4, 256), BF16),
            pltpu.VMEM((4, 2, rows // 4, 256), BF16),
            pltpu.VMEM((2, 4, 2, rows // 4, 256), F32),
            pltpu.VMEM((4, 2, rows // 4, 256), F32),
            pltpu.VMEM((4, 2, 2 * rows, 256), BF16),
            pltpu.VMEM((4, half, 2 * rows), BF16),
            pltpu.SemaphoreType.DMA((N_REMOTE,)),
            pltpu.SemaphoreType.DMA((N_REMOTE,)),
            pltpu.SemaphoreType.DMA((6,)),
            pltpu.SemaphoreType.DMA((2 * CHUNKS,)),
        ],
        compiler_params=pltpu.CompilerParams(
            collective_id=0, has_side_effects=True, vmem_limit_bytes=56 * 1024 * 1024
        ),
        cost_estimate=pl.CostEstimate(flops=6 * 10**9, bytes_accessed=20 * 10**6, transcendentals=2**18),
    )(
        pltpu.with_memory_space_constraint(tokens.reshape(4, rows // 4, depth), pltpu.HBM),
        pltpu.with_memory_space_constraint(queries[0], pltpu.HBM),
        pltpu.with_memory_space_constraint(cotangent[0], pltpu.HBM),
        pltpu.with_memory_space_constraint(key_weight, pltpu.HBM),
        pltpu.with_memory_space_constraint(value_weight, pltpu.HBM),
        probe,
    )
    return pl.pallas_call(
        store_kernel,
        out_shape=jax.ShapeDtypeStruct(result.shape, F32),
        in_specs=[pl.BlockSpec(memory_space=pltpu.VMEM)],
        out_specs=any_spec,
        scratch_shapes=[pltpu.SemaphoreType.DMA((STORES,))],
        compiler_params=pltpu.CompilerParams(vmem_limit_bytes=4 * 1024 * 1024),
        cost_estimate=pl.CostEstimate(flops=0, bytes_accessed=8 * 10**6, transcendentals=0),
    )(result)


def head_rows(block, head_index, group):
    width = group * HEAD_DIM
    return block[:, head_index * width : (head_index + 1) * width].reshape(-1, HEAD_DIM)


def forward_stats(query_rows, cot_rows, head_context, query_start, block, block_count, group):
    scaling = HEAD_DIM ** (-0.5)
    keys, values, tan_keys, tan_values = head_context
    row_count = query_rows.shape[0]
    query_pos = query_start + jnp.arange(row_count, dtype=jnp.int32) // group

    def masked_scores(block_index):
        offset = block_index * block
        key_block = lax.dynamic_slice_in_dim(keys, offset, block, 0)
        key_pos = offset + jnp.arange(block, dtype=jnp.int32)
        valid = key_pos[None, :] <= query_pos[:, None]
        return (jnp.where(valid, scaling * times_t(query_rows, key_block), NEG_FILL), offset)

    def peak_step(block_index, peak):
        scores, offset = masked_scores(block_index)
        return jnp.maximum(peak, jnp.max(scores, axis=1))

    peak = lax.fori_loop(0, block_count, peak_step, jnp.full((row_count,), NEG_FILL, jnp.float32))

    def accumulate(block_index, carry):
        total, along, acc_value, acc_mixed, acc_tan = carry
        scores, offset = masked_scores(block_index)
        tan_scores = scaling * times_t(
            query_rows, lax.dynamic_slice_in_dim(tan_keys, offset, block, 0)
        )
        value_block = lax.dynamic_slice_in_dim(values, offset, block, 0)
        tan_value_block = lax.dynamic_slice_in_dim(tan_values, offset, block, 0)
        expo = jnp.exp(scores - peak[:, None])
        expo_half = expo.astype(jnp.bfloat16)
        total = total + jnp.sum(expo, axis=1)
        along = along + jnp.sum(expo * tan_scores, axis=1)
        acc_value = acc_value + jnp.dot(expo_half, value_block, preferred_element_type=jnp.float32)
        acc_mixed = acc_mixed + jnp.dot(
            (expo * tan_scores).astype(jnp.bfloat16),
            value_block,
            preferred_element_type=jnp.float32,
        )
        acc_tan = acc_tan + jnp.dot(expo_half, tan_value_block, preferred_element_type=jnp.float32)
        return (total, along, acc_value, acc_mixed, acc_tan)

    row_zero = jnp.zeros((row_count,), jnp.float32)
    block_zero = jnp.zeros((row_count, HEAD_DIM), jnp.float32)
    total, along, acc_value, acc_mixed, acc_tan = lax.fori_loop(
        0, block_count, accumulate, (row_zero, row_zero, block_zero, block_zero, block_zero)
    )
    output = acc_value / total[:, None]
    shift_mean = along / total
    tan_output = (acc_mixed - shift_mean[:, None] * acc_value) / total[:, None] + acc_tan / total[
        :, None
    ]
    cot_float = cot_rows.astype(jnp.float32)
    delta = jnp.sum(cot_float * output, axis=1)
    tan_delta = jnp.sum(cot_float * tan_output, axis=1)
    return (peak, total, shift_mean, delta, tan_delta)


def pair_terms(query_block, cot_block, stats, query_start, kv_block, key_start, group, local_kv):
    scaling = HEAD_DIM ** (-0.5)
    query_count = query_block.shape[0]
    key_count = kv_block[0].shape[0]

    def compute():
        key_parts = []
        value_parts = []
        for head_index in range(local_kv):
            columns = slice(head_index * HEAD_DIM, (head_index + 1) * HEAD_DIM)
            keys = kv_block[0][:, columns]
            values = kv_block[1][:, columns]
            tan_keys = kv_block[2][:, columns]
            tan_values = kv_block[3][:, columns]
            query_rows = head_rows(query_block, head_index, group)
            cot_rows = head_rows(cot_block, head_index, group)
            peak, total, shift_mean, delta, tan_delta = tuple(
                (
                    item[:, head_index * group : (head_index + 1) * group].reshape(-1)
                    for item in stats
                )
            )
            query_pos = query_start + jnp.arange(query_count * group, dtype=jnp.int32) // group
            key_pos = jnp.arange(key_count, dtype=jnp.int32)
            valid = key_pos[None, :] <= query_pos[:, None]
            scores = jnp.where(valid, scaling * times_t(query_rows, keys), NEG_FILL)
            tan_scores = scaling * times_t(query_rows, tan_keys)
            probs = jnp.exp(scores - peak[:, None]) / total[:, None]
            tan_probs = probs * (tan_scores - shift_mean[:, None])
            value_parts.append(times_tn(tan_probs.astype(jnp.bfloat16), cot_rows))
            dprob = times_t(cot_rows, values)
            tan_dprob = times_t(cot_rows, tan_values)
            tan_dscore = tan_probs * (dprob - delta[:, None]) + probs * (
                tan_dprob - tan_delta[:, None]
            )
            key_parts.append(scaling * times_tn(tan_dscore.astype(jnp.bfloat16), query_rows))
        return jnp.concatenate(key_parts + value_parts, axis=1)

    def nothing():
        return jnp.zeros((key_count, 2 * local_kv * HEAD_DIM), jnp.float32)

    return lax.cond(key_start <= query_start + query_count - 1, compute, nothing)


def local(tokens, queries, cotangent, key_weight, value_weight, probe):
    tok = tokens[0]
    query_local = queries[0]
    cot_local = cotangent[0]
    tok_rows = tok.shape[0]
    model_dim = tok.shape[1]
    width = key_weight.shape[1]
    local_kv = width // HEAD_DIM
    group = HEADS // KV_HEADS
    sign = probe.astype(jnp.float32).astype(jnp.bfloat16)
    ctx_size = lax.axis_size("ctx")
    position = lax.axis_index("ctx")
    columns = tok
    sign_key = sign[0]
    sign_value = sign[1]
    projected = (
        jnp.dot(
            columns,
            lax.all_gather(key_weight, "ctx", axis=0, tiled=True),
            preferred_element_type=jnp.float32,
        ),
        jnp.dot(
            columns,
            lax.all_gather(value_weight, "ctx", axis=0, tiled=True),
            preferred_element_type=jnp.float32,
        ),
        jnp.dot(columns, sign_key, preferred_element_type=jnp.float32),
        jnp.dot(columns, sign_value, preferred_element_type=jnp.float32),
    )
    own_keys, own_values, own_tan_keys, own_tan_values = tuple(
        (item.astype(jnp.bfloat16) for item in projected)
    )
    context = (
        lax.all_gather(own_keys, "ctx", axis=0, tiled=True),
        lax.all_gather(own_values, "ctx", axis=0, tiled=True),
        lax.all_gather(own_tan_keys, "ctx", axis=0, tiled=True),
        lax.all_gather(own_tan_values, "ctx", axis=0, tiled=True),
    )
    per_block = 1
    while per_block * 2 <= max(1, 512 // tok_rows) and ctx_size % (per_block * 2) == 0:
        per_block = per_block * 2
    block = per_block * tok_rows
    query_start = position * tok_rows
    block_count = (query_start + tok_rows - 1) // block + 1
    stat_lists = ([], [], [], [], [])
    for head_index in range(local_kv):
        head_context = tuple(
            (item[:, head_index * HEAD_DIM : (head_index + 1) * HEAD_DIM] for item in context)
        )
        results = forward_stats(
            head_rows(query_local, head_index, group),
            head_rows(cot_local, head_index, group),
            head_context,
            query_start,
            block,
            block_count,
            group,
        )
        for member in range(5):
            stat_lists[member].append(results[member].reshape(tok_rows, group))
    stat_peak, stat_total, stat_shift, stat_delta, stat_tan_delta = tuple(
        (jnp.concatenate(items, axis=1) for items in stat_lists)
    )
    stats = (stat_peak, stat_total, stat_shift, stat_delta, stat_tan_delta)
    kv_block = tuple((item for item in context))
    terms = lax.psum_scatter(
        pair_terms(
            query_local, cot_local, stats, query_start, kv_block, jnp.int32(0), group, local_kv
        ),
        "ctx",
        scatter_dimension=0,
        tiled=True,
    )
    grads = terms.astype(jnp.bfloat16)
    own_rows = model_dim // ctx_size
    columns = tok
    partial_hvp = lax.psum_scatter(times_tn(columns, grads), "ctx", scatter_dimension=0, tiled=True)
    hvp = lax.psum(partial_hvp, "rep")
    hvp = hvp.reshape(own_rows, 2, width).transpose(1, 0, 2)
    sign_rows = lax.dynamic_slice_in_dim(probe, position * own_rows, own_rows, 1).astype(
        jnp.float32
    )
    return sign_rows * hvp


def fits(mesh, tokens):
    sizes = mesh.shape
    return (
        sizes["ctx"] == 2
        and sizes["head"] == 4
        and sizes["rep"] == 4
        and tokens.shape[0] == 4
        and tokens.shape[1] == 256
        and tokens.shape[2] == 4096
    )


def solution(mesh):
    def run(*arguments):
        return mapped(mesh, fused if fits(mesh, arguments[0]) else local)(*arguments)

    return run


def mapped(mesh, body):
    return jax.shard_map(
        body,
        mesh=mesh,
        in_specs=(
            P("rep", "ctx", None),
            P("rep", "ctx", "head"),
            P("rep", "ctx", "head"),
            P("ctx", "head"),
            P("ctx", "head"),
            P(None, None, "head"),
        ),
        out_specs=P(None, "ctx", "head"),
        check_vma=False,
    )
```
